256 devices in a mesh: dp: 2 (over y_lo), chan: 16 (over z, core), tm: 8 (over y_hi, x).
Axes of the slice: x: 4, y: 4 (y_hi: 2, y_lo: 2; y = y_hi * 2 + y_lo), z: 8, core: 2. Of those that a mesh axis runs over, the one named last changes fastest.
Arguments:
- features: bfloat16 [4, 16, 1024, 768], P('dp', 'chan', 'tm'), may hold values from -6 to 6
- lengths: int32 [4], P('dp'), may hold values from 256 to 1024, as said below
- chan_valid: int32 [4, 16], P('dp'), may hold values from 0 to 1, as said below
- norm_gains: float32 [3, 768], replicated, may hold values from 0.1 to 1.9
- branch_qkv: bfloat16 [768, 2304], replicated, may hold values from -32 to 32, as said below
- branch_out: bfloat16 [768, 768], replicated, may hold values from -0.6484375 to 0.6484375
- depth_taps: bfloat16 [31, 768], replicated, may hold values from -1 to 1
- point_in: bfloat16 [768, 1536], P(('dp', 'chan')), may hold values from -0.21875 to 0.21875
- point_out: bfloat16 [768, 768], P(('dp', 'chan')), may hold values from -0.21875 to 0.21875
- merge_qkv: bfloat16 [768, 2304], P(('dp', 'chan')), may hold values from -32 to 32, as said below
- merge_out: bfloat16 [768, 768], P(('dp', 'chan')), may hold values from -0.21875 to 0.21875
Outputs:
- merged: bfloat16 [4, 16, 1024, 768], P('dp', 'chan', 'tm')
The draws below stay inside these ranges and needn't reach their ends.
Inputs may be any that keep to these rules, and one draw needn't show every extreme that they name: `lengths`: one utterance has all 1024 frames valid and one has at most 512. `chan_valid`: every utterance has one or more working channels. `branch_qkv`: entries of order 768^-0.5. `merge_qkv`: entries of order 768^-0.5.
All inputs are finite; a program needn't handle non-finite values.
Results may differ from the reference program's by a relative error of at most 0.018.
Values may be sent and summed in bfloat16 or wider, within the bound.
No kernel may reach another device: no remote copies, remote signals or barrier semaphores. Data moves between devices by JAX's collectives and lax.ppermute only.
A program may use at most 128 MiB of HBM per device.

```python
import jax
import jax.numpy as jnp
from jax import lax

D = 768
HEADS = 12
HD = 64
KER = 31
HALF = 15
UTT = 4
CHANNELS = 16
FRAMES = 1024


def drawn_matrix(key):
    drawn = jax.random.normal(key, (D, 3 * D), jnp.float32)
    return jnp.clip(drawn, -6.0, 6.0) * D ** (-0.5)


def draw_branch_qkv(key, part):
    key = jax.random.fold_in(key, 11)
    return drawn_matrix(key).astype(jnp.bfloat16)


def draw_merge_qkv(key, part):
    key = jax.random.fold_in(key, 12)
    return drawn_matrix(key).astype(jnp.bfloat16)


def draw_lengths(key, part):
    key = jax.random.fold_in(key, 5)
    first_key, second_key, third_key = jax.random.split(key, 3)
    drawn = jax.random.randint(first_key, (UTT,), FRAMES // 4, FRAMES + 1, jnp.int32)
    order = jax.random.permutation(second_key, UTT)
    short_len = jax.random.randint(third_key, (), FRAMES // 4, FRAMES // 2 + 1, jnp.int32)
    drawn = drawn.at[order[0]].set(FRAMES)
    drawn = drawn.at[order[1]].set(short_len)
    return drawn.astype(jnp.int32)


def draw_chan_valid(key, part):
    key = jax.random.fold_in(key, 7)
    first_key, second_key = jax.random.split(key)
    flags = (jax.random.randint(first_key, (UTT, CHANNELS), 0, 4, jnp.int32) < 3).astype(jnp.int32)
    chosen = jax.random.randint(second_key, (UTT,), 0, CHANNELS, jnp.int32)
    marked = jnp.arange(CHANNELS, dtype=jnp.int32)[None, :] == chosen[:, None]
    return jnp.where(marked, 1, flags).astype(jnp.int32)


def level_of(key, extent, cuts, low, high):
    level, own = 1.0, jax.random.fold_in(key, 6)
    for dim, shards_of in cuts:
        heights = jnp.exp(jax.random.uniform(jax.random.fold_in(own, dim), (shards_of,), jnp.float32, low / len(cuts), high / len(cuts)))
        level = level * jnp.repeat(heights, extent[dim] // shards_of).reshape([-1 if axis == dim else 1 for axis in range(len(extent))])
    return level


def normal_values(stream_key, shape, deviation, most, pieces=(), held_as=jnp.bfloat16):
    level = level_of(stream_key, shape, pieces, -0.22, 0.18) if pieces else 1.0
    entries = jax.random.normal(stream_key, shape, jnp.float32) * deviation * level
    return jnp.minimum(jnp.maximum(entries, -most), most).astype(held_as)


def setup_inputs(seed: int = 0) -> dict:
    key_list = jax.random.split(jax.random.key(seed), 12)
    return {
        "features": normal_values(key_list[0], (UTT, CHANNELS, FRAMES, D), 1.0, 6.0, ((0, 2), (1, 16), (2, 8))),
        "lengths": draw_lengths(jax.random.fold_in(key_list[11], 71), 0),
        "chan_valid": draw_chan_valid(jax.random.fold_in(key_list[11], 71), 0),
        "norm_gains": jnp.clip(1.0 + 0.18 * jax.random.normal(key_list[3], (3, D), jnp.float32), 0.1, 1.9),
        "branch_qkv": draw_branch_qkv(jax.random.fold_in(key_list[11], 71), 0),
        "branch_out": normal_values(key_list[5], (D, D), (3 * D ** -0.5), 0.6484375),
        "depth_taps": normal_values(key_list[6], (KER, D), KER ** -0.5, 1.0),
        "point_in": normal_values(key_list[7], (D, 2 * D), D ** -0.5, 0.21875, ((0, 32),)),
        "point_out": normal_values(key_list[8], (D, D), D ** -0.5, 0.21875, ((0, 32),)),
        "merge_qkv": draw_merge_qkv(jax.random.fold_in(key_list[11], 71), 0),
        "merge_out": normal_values(key_list[10], (D, D), D ** -0.5, 0.21875, ((0, 32),)),
    }


def layer_norm(values, gain):
    data = values.astype(jnp.float32)
    center = data - lax.optimization_barrier(jnp.mean(data, axis=-1, keepdims=True))
    spread = lax.optimization_barrier(jnp.mean(center * center, axis=-1, keepdims=True))
    return center * lax.rsqrt(spread + 1e-05) * gain

def branch_layer(inputs, frame_live, norm_gains, branch_qkv, branch_out, depth_taps, point_in, point_out):
    normed = layer_norm(inputs, norm_gains[0]).astype(jnp.bfloat16)
    project = jnp.dot(normed, branch_qkv, preferred_element_type=jnp.float32).astype(jnp.bfloat16)
    query = project[:, :D].reshape(FRAMES, HEADS, HD).astype(jnp.float32)
    keyed = project[:, D:2 * D].reshape(FRAMES, HEADS, HD).astype(jnp.float32)
    valued = project[:, 2 * D:].reshape(FRAMES, HEADS, HD).astype(jnp.float32)
    scores = jnp.einsum('qhd,khd->hqk', query, keyed) * HD ** (-0.5)
    scores = jnp.where(frame_live[None, None, :], scores, -1e+30)
    attend = jax.nn.softmax(scores, axis=-1).astype(jnp.bfloat16)
    context = jnp.einsum('hqk,khd->qhd', attend.astype(jnp.float32), valued).astype(jnp.bfloat16).reshape(FRAMES, D)
    first = (inputs.astype(jnp.float32) + jnp.dot(context, branch_out, preferred_element_type=jnp.float32)).astype(jnp.bfloat16)
    normed_two = layer_norm(first, norm_gains[1]).astype(jnp.bfloat16)
    widened = jnp.dot(normed_two, point_in, preferred_element_type=jnp.float32)
    gated = jnp.where(frame_live[:, None], widened[:, :D] * jax.nn.sigmoid(widened[:, D:]), 0.0).astype(jnp.bfloat16)
    padded = jnp.pad(gated.astype(jnp.float32), ((HALF, HALF), (0, 0)))
    taps = depth_taps.astype(jnp.float32)
    mixed = jnp.zeros((FRAMES, D), jnp.float32)
    for offset in range(KER):
        mixed = mixed + taps[offset] * padded[offset:offset + FRAMES]
    swished = jax.nn.silu(mixed).astype(jnp.bfloat16)
    return (first.astype(jnp.float32) + jnp.dot(swished, point_out, preferred_element_type=jnp.float32)).astype(jnp.bfloat16)

def merge_utterance(block, channel_live, norm_gains, merge_qkv, merge_out):
    normed = layer_norm(block, norm_gains[2]).astype(jnp.bfloat16).reshape(CHANNELS * FRAMES, D)
    project = jnp.dot(normed, merge_qkv, preferred_element_type=jnp.float32).astype(jnp.bfloat16)
    project = project.reshape(CHANNELS, FRAMES, 3 * D)
    query = project[..., :D].reshape(CHANNELS, FRAMES, HEADS, HD).astype(jnp.float32)
    keyed = project[..., D:2 * D].reshape(CHANNELS, FRAMES, HEADS, HD).astype(jnp.float32)
    valued = project[..., 2 * D:].reshape(CHANNELS, FRAMES, HEADS, HD).astype(jnp.float32)
    scores = jnp.einsum('cfhd,efhd->fhce', query, keyed) * HD ** (-0.5)
    scores = jnp.where(channel_live[None, None, None, :] > 0, scores, -1e+30)
    attend = jax.nn.softmax(scores, axis=-1).astype(jnp.bfloat16)
    context = jnp.einsum('fhce,efhd->cfhd', attend.astype(jnp.float32), valued).astype(jnp.bfloat16)
    context = context.reshape(CHANNELS * FRAMES, D)
    result = block.reshape(CHANNELS * FRAMES, D).astype(jnp.float32) + jnp.dot(context, merge_out, preferred_element_type=jnp.float32)
    return result.astype(jnp.bfloat16).reshape(CHANNELS, FRAMES, D)

def reference(features, lengths, chan_valid, norm_gains, branch_qkv, branch_out, depth_taps, point_in, point_out, merge_qkv, merge_out):
    frame_live = jnp.arange(FRAMES, dtype=jnp.int32)[None, :] < lengths[:, None]
    flat = features.reshape(UTT * CHANNELS, FRAMES, D)
    live_rows = jnp.repeat(frame_live, CHANNELS, axis=0)

    def run_branch(packed):
        return branch_layer(packed[0], packed[1], norm_gains, branch_qkv, branch_out, depth_taps, point_in, point_out)
    branched = lax.map(run_branch, (flat, live_rows)).reshape(UTT, CHANNELS, FRAMES, D)

    def run_merging(packed):
        return merge_utterance(packed[0], packed[1], norm_gains, merge_qkv, merge_out)
    return lax.map(run_merging, (branched, chan_valid))
```

```python
import functools

import jax
import jax.numpy as jnp
from jax import lax
from jax.experimental import pallas as pl
from jax.experimental.pallas import tpu as pltpu
from jax.sharding import PartitionSpec as P

D = 768
PAIRS = 6
SPAN = 128
PAD = 16
SEG = SPAN + 2 * PAD
FRAMES = 1024
ROWS = 4
TAPS = 31
MIB = 1024 * 1024
LOG2E = 1.4426950408889634


def normalize(values, gain):
    data = values.astype(jnp.float32)
    center = data - jnp.mean(data, axis=-1, keepdims=True)
    spread = jnp.mean(center * center, axis=-1, keepdims=True)
    return (center * lax.rsqrt(spread + 1e-05) * gain).astype(jnp.bfloat16)


def mm(left, right):
    return jnp.dot(left, right, preferred_element_type=jnp.float32)


def mm_t(left, right):
    return lax.dot_general(left, right, (((1,), (1,)), ((), ())), preferred_element_type=jnp.float32)


def pair_attention(query, key, value_ones, allowed):
    low = lax.broadcasted_iota(jnp.int32, query.shape, 1) < 64
    zero = jnp.zeros_like(query)
    outs = []
    for one in (jnp.where(low, query, zero), jnp.where(low, zero, query)):
        scores = jnp.where(allowed, mm_t(one, key), -1e30)
        top = jnp.max(scores, axis=1, keepdims=True)
        weights = jnp.exp2((scores - top) * LOG2E).astype(jnp.bfloat16)
        out = mm(weights, value_ones)
        outs.append(out[:, :128] / out[:, 128:])
    return jnp.where(low, outs[0], outs[1]).astype(jnp.bfloat16)


def branch_kernel(
    where_ref, h0, h1, h3, h2, g0, g1, g3, g2, gains, wq, wk, wv, wout,
    first_ref, normed_ref, norm_s, raw_s, query_s, context_s,
):
    step = pl.program_id(0)
    col, row, length = where_ref[0], where_ref[1], where_ref[2]
    blocks = (h0, h1, h3, h2, g0, g1, g3, g2)

    @pl.when(step == 0)
    def _():
        for j, block in enumerate(blocks):
            norm_s[j * SPAN : (j + 1) * SPAN] = normalize(block[...], gains[0:1])
        inner_right, inner_left = col < ROWS - 1, col > 0

        def lay(dst, read):
            dst[PAD : PAD + SPAN] = read(0, 0, SPAN)
            dst[SEG + PAD : SEG + PAD + SPAN] = read(4, 0, SPAN)
            last, lo = SPAN - PAD, SPAN
            prev_h, prev_g = read(1, last, SPAN), read(5, last, SPAN)
            next_h, next_g = read(2, 0, PAD), read(6, 0, PAD)
            dst[0:PAD] = jnp.where(inner_left, prev_h, prev_g)
            dst[SEG : SEG + PAD] = jnp.where(inner_left, prev_g, prev_h)
            dst[PAD + SPAN : SEG] = jnp.where(inner_right, next_h, next_g)
            dst[SEG + PAD + SPAN :] = jnp.where(inner_right, next_g, next_h)

        lay(raw_s, lambda j, a, b: blocks[j][a:b])
        lay(query_s, lambda j, a, b: norm_s[j * SPAN + a : j * SPAN + b])

    both = mm(norm_s[...], jnp.concatenate([wk[...], wv[...]], axis=1)).astype(jnp.bfloat16)
    key, value = both[:, :128], both[:, 128:]
    value_ones = jnp.concatenate([value, jnp.ones_like(value)], axis=1)
    query = mm(query_s[...], wq[...]).astype(jnp.bfloat16) * jnp.bfloat16(0.125)
    lane = lax.broadcasted_iota(jnp.int32, (1, SPAN), 1)
    starts = []
    for r in (row, 1 - row):
        for k in (0, 1, 3, 2):
            starts.append((r * ROWS + lax.rem(col + ROWS - k, ROWS)) * SPAN)
    allowed = jnp.concatenate([lane + s for s in starts], axis=1) < length
    columns = pl.ds(pl.multiple_of(step * 128, 128), 128)
    for seg in range(2):
        at = slice(seg * SEG, (seg + 1) * SEG)
        context_s[at, columns] = pair_attention(query[at], key, value_ones, allowed)

    @pl.when(step == PAIRS - 1)
    def _():
        first = (raw_s[...].astype(jnp.float32) + mm(context_s[...], wout[...])).astype(jnp.bfloat16)
        first_ref[...] = first
        normed_ref[...] = normalize(first, gains[1:2])


def run_branch(where, blocks, gains, qkv, wout):
    whole = lambda shape: pl.BlockSpec(shape, lambda p: (0,) * len(shape))
    return pl.pallas_call(
        branch_kernel,
        grid=(PAIRS,),
        in_specs=[pl.BlockSpec(memory_space=pltpu.SMEM)]
        + [whole((SPAN, D))] * 8
        + [
            whole((3, D)),
            pl.BlockSpec((D, 128), lambda p: (0, p)),
            pl.BlockSpec((D, 128), lambda p: (0, PAIRS + p)),
            pl.BlockSpec((D, 128), lambda p: (0, 2 * PAIRS + p)),
            whole((D, D)),
        ],
        out_specs=[whole((2 * SEG, D))] * 2,
        out_shape=[jax.ShapeDtypeStruct((2 * SEG, D), jnp.bfloat16)] * 2,
        scratch_shapes=[
            pltpu.VMEM((FRAMES, D), jnp.bfloat16),
            pltpu.VMEM((2 * SEG, D), jnp.bfloat16),
            pltpu.VMEM((2 * SEG, D), jnp.bfloat16),
            pltpu.VMEM((2 * SEG, D), jnp.bfloat16),
        ],
        compiler_params=pltpu.CompilerParams(vmem_limit_bytes=48 * MIB),
        cost_estimate=pl.CostEstimate(
            flops=6 * 10**9, bytes_accessed=8 * 10**6, transcendentals=4 * 10**6
        ),
        name="branch",
    )(where, *blocks, gains, qkv, qkv, qkv, wout)


def conv_kernel(where_ref, normed, first, wide, back, taps, out_ref, gated_s, swish_s):
    col, row, length = where_ref[0], where_ref[1], where_ref[2]
    for seg in range(2):
        at = slice(seg * SEG, (seg + 1) * SEG)
        begin = ((row if seg == 0 else 1 - row) * ROWS + col) * SPAN - PAD
        frame = begin + lax.broadcasted_iota(jnp.int32, (SEG, 1), 0)
        live = (frame >= 0) & (frame < length)
        rows = normed[at]
        for chunk in range(PAIRS):
            lo = chunk * 128
            value = mm(rows, wide[:, lo : lo + 128])
            gate = mm(rows, wide[:, D + lo : D + lo + 128])
            gated = jnp.where(live, value * jax.nn.sigmoid(gate), 0.0)
            gated_s[chunk, at] = gated.astype(jnp.bfloat16).astype(jnp.float32)
    for seg in range(2):
        for chunk in range(PAIRS):
            lo = chunk * 128
            mixed = jnp.zeros((SPAN, 128), jnp.float32)
            for o in range(TAPS):
                begin = seg * SEG + PAD - TAPS // 2 + o
                tap = taps[o : o + 1, lo : lo + 128]
                mixed = mixed + tap * gated_s[chunk, begin : begin + SPAN]
            swish = mixed * jax.nn.sigmoid(mixed)
            swish_s[seg * SPAN : (seg + 1) * SPAN, lo : lo + 128] = swish.astype(jnp.bfloat16)
    out = mm(swish_s[...], back[...])
    for seg in range(2):
        kept = first[seg * SEG + PAD : seg * SEG + PAD + SPAN].astype(jnp.float32)
        out_ref[seg * SPAN : (seg + 1) * SPAN] = (
            kept + out[seg * SPAN : (seg + 1) * SPAN]
        ).astype(jnp.bfloat16)


def run_conv(where, normed, first, weights, taps):
    return pl.pallas_call(
        conv_kernel,
        grid=(1,),
        in_specs=[
            pl.BlockSpec(memory_space=pltpu.SMEM),
            pl.BlockSpec((2 * SEG, D), lambda i: (0, 0)),
            pl.BlockSpec((2 * SEG, D), lambda i: (0, 0)),
            pl.BlockSpec((D, 2 * D), lambda i: (0, 0)),
            pl.BlockSpec((D, D), lambda i: (0, 2)),
            pl.BlockSpec((TAPS, D), lambda i: (0, 0)),
        ],
        out_specs=pl.BlockSpec((2 * SPAN, D), lambda i: (0, 0)),
        out_shape=jax.ShapeDtypeStruct((2 * SPAN, D), jnp.bfloat16),
        scratch_shapes=[
            pltpu.VMEM((PAIRS, 2 * SEG, 128), jnp.float32),
            pltpu.VMEM((2 * SPAN, D), jnp.bfloat16),
        ],
        compiler_params=pltpu.CompilerParams(vmem_limit_bytes=48 * MIB),
        cost_estimate=pl.CostEstimate(
            flops=2 * 10**9, bytes_accessed=8 * 10**6, transcendentals=10**6
        ),
        name="conv",
    )(where, normed, first, weights, weights, taps)


def merge_kernel(live, block, gains, wq, wk, wv, wout, out_ref, norm_s, context_s):
    step = pl.program_id(0)

    @pl.when(step == 0)
    def _():
        norm_s[...] = normalize(block[...], gains[2:3])

    projected = mm(norm_s[...], jnp.concatenate([wk[...], wv[...]], axis=1)).astype(jnp.bfloat16)
    key, value = projected[:, :128], projected[:, 128:]
    value_ones = jnp.concatenate([value, jnp.ones_like(value)], axis=1)
    query = mm(norm_s[...], wq[...]).astype(jnp.bfloat16) * jnp.bfloat16(0.125)
    count = block.shape[0]
    mine = lax.broadcasted_iota(jnp.int32, (count, count), 0) & 15
    theirs = lax.broadcasted_iota(jnp.int32, (count, count), 1) & 15
    allowed = (mine == theirs) & (live[...] > 0)
    columns = pl.ds(pl.multiple_of(step * 128, 128), 128)
    context_s[:, columns] = pair_attention(query, key, value_ones, allowed)

    @pl.when(step == PAIRS - 1)
    def _():
        out = block[...].astype(jnp.float32) + mm(context_s[...], wout[...])
        out_ref[...] = out.astype(jnp.bfloat16)


def run_merge(live, block, gains, weights, first_column):
    whole = lambda shape: pl.BlockSpec(shape, lambda p: (0,) * len(shape))
    count = block.shape[0]
    base = first_column // 128
    return pl.pallas_call(
        merge_kernel,
        grid=(PAIRS,),
        in_specs=[
            whole((1, count)),
            whole((count, D)),
            whole((3, D)),
            pl.BlockSpec((D, 128), lambda p: (0, base + p)),
            pl.BlockSpec((D, 128), lambda p: (0, base + PAIRS + p)),
            pl.BlockSpec((D, 128), lambda p: (0, base + 2 * PAIRS + p)),
            pl.BlockSpec((D, D), lambda p: (0, base // PAIRS + 3)),
        ],
        out_specs=whole((count, D)),
        out_shape=jax.ShapeDtypeStruct((count, D), jnp.bfloat16),
        scratch_shapes=[
            pltpu.VMEM((count, D), jnp.bfloat16),
            pltpu.VMEM((count, D), jnp.bfloat16),
        ],
        compiler_params=pltpu.CompilerParams(vmem_limit_bytes=48 * MIB),
        cost_estimate=pl.CostEstimate(
            flops=2 * 10**9, bytes_accessed=8 * 10**6, transcendentals=10**6
        ),
        name="merge",
    )(live, block, gains, weights, weights, weights, weights)


def shards(
    features, lengths, chan_valid, norm_gains, branch_qkv, branch_out, depth_taps,
    point_in, point_out, merge_qkv, merge_out,
):
    place = lax.axis_index("tm")
    row, col = place // ROWS, place % ROWS
    count = 2 * ROWS
    packed = jnp.concatenate([point_in, point_out, merge_qkv, merge_out], axis=1)
    weights = lax.all_gather(packed, ("dp", "chan"), axis=0, tiled=True)

    other_row = [(i, (i + ROWS) % count) for i in range(count)]

    def along(values, k):
        return lax.ppermute(
            values, "tm", [(i, i // ROWS * ROWS + (i + k) % ROWS) for i in range(count)]
        )

    home = lax.dynamic_index_in_dim(features[:, 0], row, 0, keepdims=False)
    away = lax.dynamic_index_in_dim(features[:, 0], 1 - row, 0, keepdims=False)
    swapped = lax.ppermute(away, "tm", other_row)
    blocks = [home] + [along(home, k) for k in (1, 3, 2)]
    blocks += [swapped] + [along(swapped, k) for k in (1, 3, 2)]
    where = jnp.stack([col, row, lengths[row]]).astype(jnp.int32)
    first, normed = run_branch(where, blocks, norm_gains, branch_qkv, branch_out)
    second = run_conv(where, normed, first, weights, depth_taps.astype(jnp.float32))
    back = lax.ppermute(second[SPAN:], "tm", other_row)
    second = jnp.concatenate([second[:SPAN], back], axis=0)
    channels = lax.axis_size("chan")
    part = 2 * SPAN // channels
    joined = lax.all_to_all(
        second.reshape(channels, part, D), "chan", split_axis=0, concat_axis=0, tiled=True
    )
    mine = jnp.where(lax.axis_index("chan") < channels // 2, row, 1 - row)
    live = jnp.repeat(chan_valid[mine], part)[None]
    merged = run_merge(live, joined.reshape(channels * part, D), norm_gains, weights, 3 * D)
    returned = lax.all_to_all(
        merged.reshape(channels, part, D), "chan", split_axis=0, concat_axis=0, tiled=True
    ).reshape(2, SPAN, D)
    return jnp.where(row == 0, returned, returned[::-1])[:, None]


def solution(mesh):
    placed = (
        P("dp", "chan", "tm", None),
        P("dp"),
        P("dp", None),
        P(),
        P(),
        P(),
        P(),
        P(("dp", "chan"), None),
        P(("dp", "chan"), None),
        P(("dp", "chan"), None),
        P(("dp", "chan"), None),
    )
    return jax.shard_map(
        shards, mesh=mesh, in_specs=placed, out_specs=P("dp", "chan", "tm", None), check_vma=False
    )
```

```python
import jax
import jax.numpy as jnp
from jax import lax
from jax.experimental import pallas as pl
from jax.experimental.pallas import tpu as pltpu
from jax.sharding import PartitionSpec as P

D = 768
PAIRS = 6
SPAN = 128
PAD = 16
SEG = SPAN + 2 * PAD
FRAMES = 1024
ROWS = 4
TAPS = 31
MIB = 1024 * 1024
LOG2E = 1.4426950408889634


def normalize(values, gain):
    data = values.astype(jnp.float32)
    center = data - jnp.mean(data, axis=-1, keepdims=True)
    spread = jnp.mean(center * center, axis=-1, keepdims=True)
    return (center * lax.rsqrt(spread + 1e-05) * gain).astype(jnp.bfloat16)


def mm(left, right):
    return jnp.dot(left, right, preferred_element_type=jnp.float32)


def mm_t(left, right):
    return lax.dot_general(left, right, (((1,), (1,)), ((), ())), preferred_element_type=jnp.float32)


def pair_attention(query, key, value_ones, allowed):
    low = lax.broadcasted_iota(jnp.int32, query.shape, 1) < 64
    zero = jnp.zeros_like(query)
    outs = []
    for one in (jnp.where(low, query, zero), jnp.where(low, zero, query)):
        scores = jnp.where(allowed, mm_t(one, key), -1e30)
        top = jnp.max(scores, axis=1, keepdims=True)
        weights = jnp.exp2((scores - top) * LOG2E).astype(jnp.bfloat16)
        out = mm(weights, value_ones)
        outs.append(out[:, :128] / out[:, 128:])
    return jnp.where(low, outs[0], outs[1]).astype(jnp.bfloat16)


def with_ones(both):
    value = both[:, 128:]
    return both[:, :128], jnp.concatenate([value, jnp.ones_like(value)], axis=1)


def bf16(*shape):
    return jax.ShapeDtypeStruct(shape, jnp.bfloat16)


def call(kernel, outs, scratch, cost, name, operands, where=None, limit=24):
    vmem = pl.BlockSpec(memory_space=pltpu.VMEM)
    flops, moved, exps = cost
    lead = [] if where is None else [where]
    return pl.pallas_call(
        kernel,
        in_specs=[pl.BlockSpec(memory_space=pltpu.SMEM)] * len(lead)
        + [pl.BlockSpec(memory_space=pltpu.HBM) if isinstance(x, Far) else vmem for x in operands],
        out_specs=[vmem] * len(outs),
        out_shape=outs,
        scratch_shapes=scratch,
        compiler_params=pltpu.CompilerParams(vmem_limit_bytes=limit * MIB),
        cost_estimate=pl.CostEstimate(flops=flops, bytes_accessed=moved, transcendentals=exps),
        name=name,
    )(*lead, *[x.array if isinstance(x, Far) else x for x in operands])


class Far:
    def __init__(self, array):
        self.array = array


def prepare_kernel(
    pin, pout, mqkv, mout, features, out_ref, spread_ref, pin_s, pout_s, mqkv_s, mout_s, sems
):
    shards_in = ((pin, pin_s), (pout, pout_s), (mqkv, mqkv_s), (mout, mout_s))
    blocks = [(features.at[t // ROWS, 0], spread_ref.at[t]) for t in range(2 * ROWS)]
    copies = [
        pltpu.make_async_copy(a, b, sems.at[n]) for n, (a, b) in enumerate((*shards_in, *blocks))
    ]
    for copy in copies:
        copy.start()
    for copy in copies[:4]:
        copy.wait()
    half = D // 2
    col = lax.rem(lax.axis_index("tm"), ROWS)
    for h in range(2):
        lo, base = h * half, h * 2 * D
        out_ref[:, base : base + half] = pin_s[:, lo : lo + half]
        out_ref[:, base + half : base + 2 * half] = pin_s[:, D + lo : D + lo + half]
        out_ref[:, base + 2 * half : base + 3 * half] = pout_s[:, lo : lo + half]

        @pl.when(col < ROWS - 1)
        def _():
            for n in range(3):
                lanes = pl.ds(pl.multiple_of(n * D + (2 * col + h) * 128, 128), 128)
                at = base + 3 * half + n * 128
                out_ref[:, at : at + 128] = mqkv_s[:, lanes]

        @pl.when(col == ROWS - 1)
        def _():
            out_ref[:, base + 3 * half : base + 4 * half] = mout_s[:, lo : lo + half]

    for copy in copies[4:]:
        copy.wait()


def run_prepare(features, *shards_in):
    height, count = shards_in[0].shape[0], 2 * ROWS
    scratch = [pltpu.VMEM(w.shape, w.dtype) for w in shards_in]
    return call(
        prepare_kernel, [bf16(height, 4 * D), bf16(count, SPAN, D)],
        scratch + [pltpu.SemaphoreType.DMA((4 + count,))],
        (0, 3 * 10**6, 0), "prepare", [Far(w) for w in (*shards_in, features)], limit=56,
    )


def my_core():
    return lax.rem(lax.axis_index("chan"), 2)


def my_length(lengths):
    return lengths[lax.axis_index("tm") // ROWS]


def attend_pairs(length, norm_s, query_s, weights, context_ref):
    allowed = lax.broadcasted_iota(jnp.int32, (1, FRAMES), 1) < length
    query_two = mm(query_s[...], weights[:, :256]).astype(jnp.bfloat16) * jnp.bfloat16(0.125)
    for n in range(2):
        lanes = slice(n * 128, (n + 1) * 128)
        both = jnp.concatenate([weights[:, 256:512][:, lanes], weights[:, 512:][:, lanes]], axis=1)
        key, value_ones = with_ones(mm(norm_s[...], both).astype(jnp.bfloat16))
        context_ref[:, lanes] = pair_attention(query_two[:, lanes], key, value_ones, allowed)


def attend_a_kernel(
    lengths, blocks, gains, qkv, wout,
    context_ref, norm_s, query_s, raw_s, group_b, group_c, wout_ref, group_a, sems,
):
    copies = []
    for n, group in enumerate((group_a, group_b, group_c)):
        for m in range(3):
            columns = pl.ds(m * D + n * 256, 256)
            copies.append((qkv.at[:, columns], group.at[:, pl.ds(m * 256, 256)]))
    copies.append((wout, wout_ref))
    copies = [pltpu.make_async_copy(a, b, sems.at[n]) for n, (a, b) in enumerate(copies)]
    for copy in copies:
        copy.start()
    for b in range(2 * ROWS):
        norm_s[b * SPAN : (b + 1) * SPAN] = normalize(blocks[b], gains[0:1])
    count = 2 * ROWS
    place = lax.axis_index("tm")
    for seg, b in enumerate((place, lax.rem(place + ROWS, count))):
        at, start = seg * SEG, b * SPAN
        before, following = jnp.maximum(b - 1, 0), jnp.minimum(b + 1, count - 1)
        raw_s[at : at + PAD] = blocks[before, SPAN - PAD :]
        raw_s[at + PAD : at + PAD + SPAN] = blocks[b]
        raw_s[at + PAD + SPAN : at + SEG] = blocks[following, :PAD]
        rows = lambda begin, size: norm_s[pl.ds(pl.multiple_of(begin, PAD), size)]
        query_s[at : at + PAD] = rows(before * SPAN + SPAN - PAD, PAD)
        query_s[at + PAD : at + PAD + SPAN] = rows(start, SPAN)
        query_s[at + PAD + SPAN : at + SEG] = rows(following * SPAN, PAD)
    for copy in copies[:3]:
        copy.wait()
    attend_pairs(my_length(lengths), norm_s, query_s, group_a, context_ref)
    for copy in copies[3:]:
        copy.wait()


def attend_b_kernel(lengths, norm_s, query_s, weights, context_ref):
    attend_pairs(my_length(lengths), norm_s, query_s, weights, context_ref)


def attend_c_kernel(
    lengths, norm_s, query_s, raw_s, context_a, context_b, gains, weights, wout,
    first_ref, normed_ref, context_c,
):
    attend_pairs(my_length(lengths), norm_s, query_s, weights, context_c)
    third = D // 3
    out = sum(
        mm(c[...], wout[n * third : (n + 1) * third])
        for n, c in enumerate((context_a, context_b, context_c))
    )
    first = (raw_s[...].astype(jnp.float32) + out).astype(jnp.bfloat16)
    first_ref[...] = first
    normed_ref[...] = normalize(first, gains[1:2])


WIDE = 2 * SEG
ATTEND_COST = (3 * 10**9, 5 * 10**6, 10**6)


def run_attend_a(lengths, blocks, gains, qkv, wout):
    group = bf16(D, D)
    return call(
        attend_a_kernel,
        [bf16(WIDE, D // 3), bf16(FRAMES, D), bf16(WIDE, D), bf16(WIDE, D), group, group, group],
        [pltpu.VMEM((D, D), jnp.bfloat16), pltpu.SemaphoreType.DMA((10,))],
        ATTEND_COST, "attend_a", [blocks, gains, Far(qkv), Far(wout)], lengths, limit=48,
    )


def run_attend_b(lengths, norm, query, weights):
    (context,) = call(
        attend_b_kernel, [bf16(WIDE, D // 3)], [], ATTEND_COST, "attend_b", [norm, query, weights], lengths,
    )
    return context


def run_attend_c(lengths, *operands):
    return call(
        attend_c_kernel, [bf16(WIDE, D)] * 2, [pltpu.VMEM((WIDE, D // 3), jnp.bfloat16)],
        ATTEND_COST, "attend_c", list(operands), lengths,
    )


def depthwise(gated, base, taps, swish_s):
    for chunk in range(PAIRS):
        lo = chunk * 128
        mixed = jnp.zeros((SPAN, 128), jnp.float32)
        for o in range(TAPS):
            begin = base + PAD - TAPS // 2 + o
            tap = taps[o : o + 1, lo : lo + 128]
            mixed = mixed + tap * gated[chunk, begin : begin + SPAN]
        swish = mixed * jax.nn.sigmoid(mixed)
        swish_s[:, lo : lo + 128] = swish.astype(jnp.bfloat16)


def project_out(swish_s, kept, core, halves, out_ref):
    for h, half in zip((core, 1 - core), halves):
        lanes = pl.ds(pl.multiple_of(h * (D // 2), 128), D // 2)
        out = kept[:, lanes].astype(jnp.float32) + mm(swish_s[...], half[:, D:])
        out_ref[:, lanes] = out.astype(jnp.bfloat16)


def conv_a_kernel(
    lengths, normed, first, mine, other, taps, out_ref, home_ref, gated_s, swish_s, kept_s
):
    place, length, core = lax.axis_index("tm"), my_length(lengths), my_core()
    lives = []
    for b in (place, lax.rem(place + ROWS, 2 * ROWS)):
        frame = b * SPAN - PAD + lax.broadcasted_iota(jnp.int32, (SEG, 1), 0)
        lives.append((frame >= 0) & (frame < length))
    live = jnp.concatenate(lives, axis=0)
    for h, half in zip((core, 1 - core), (mine, other)):
        for n in range(PAIRS // 2):
            lo = n * 128
            both = jnp.concatenate(
                [half[:, lo : lo + 128], half[:, D // 2 + lo : D // 2 + lo + 128]], axis=1
            )
            wide = mm(normed[...], both)
            gated = jnp.where(live, wide[:, :128] * jax.nn.sigmoid(wide[:, 128:]), 0.0)
            gated = gated.astype(jnp.bfloat16).astype(jnp.float32)
            chunk = h * (PAIRS // 2) + n
            home_ref[chunk] = gated[:SEG]
            gated_s[chunk] = gated[SEG:]
    depthwise(gated_s, 0, taps, swish_s)
    kept_s[...] = first[SEG + PAD : SEG + PAD + SPAN]
    project_out(swish_s, kept_s, core, (mine, other), out_ref)


def conv_b_kernel(home, first, mine, other, taps, out_ref, swish_s, kept_s):
    depthwise(home, 0, taps, swish_s)
    kept_s[...] = first[PAD : PAD + SPAN]
    project_out(swish_s, kept_s, my_core(), (mine, other), out_ref)


def run_conv(lengths, normed, first, mine, other, taps):
    gated = jax.ShapeDtypeStruct((PAIRS, SEG, 128), jnp.float32)
    block = pltpu.VMEM((SPAN, D), jnp.bfloat16)
    away, home = call(
        conv_a_kernel, [bf16(SPAN, D), gated], [pltpu.VMEM(gated.shape, jnp.float32), block, block],
        (2 * 10**9, 6 * 10**6, 10**6), "conv_a", [normed, first, mine, other, taps], lengths,
    )
    (kept,) = call(
        conv_b_kernel, [bf16(SPAN, D)], [block, block],
        (10**9, 4 * 10**6, 10**6), "conv_b", [home, first, mine, other, taps],
    )
    return kept, away


def merge_kernel(live, block, gains, *refs):
    eighths, (out_ref, norm_s, context_s, weights_s) = refs[:8], refs[8:]
    col, core = lax.rem(lax.axis_index("tm"), ROWS), my_core()
    for n, eighth in enumerate(eighths):
        k = (0, 1, 3, 2)[n % 4]
        e = 2 * lax.rem(col + ROWS - k, ROWS) + (core if n < 4 else 1 - core)
        weights_s[e] = eighth[...]
    norm_s[...] = normalize(block[...], gains[2:3])
    count = block.shape[0]
    mine = lax.broadcasted_iota(jnp.int32, (count, count), 0) & 15
    theirs = lax.broadcasted_iota(jnp.int32, (count, count), 1) & 15
    allowed = (mine == theirs) & (live[...] > 0)
    for p in range(PAIRS):
        key, value_ones = with_ones(mm(norm_s[...], weights_s[p, :, 128:]).astype(jnp.bfloat16))
        query = mm(norm_s[...], weights_s[p, :, :128]).astype(jnp.bfloat16) * jnp.bfloat16(0.125)
        context_s[:, p * 128 : (p + 1) * 128] = pair_attention(query, key, value_ones, allowed)
    for n in range(2):
        lanes = slice(n * (D // 2), (n + 1) * (D // 2))
        out = block[:, lanes].astype(jnp.float32) + mm(context_s[...], weights_s[PAIRS + n])
        out_ref[:, lanes] = out.astype(jnp.bfloat16)


def run_merge(live, block, gains, eighths):
    count = block.shape[0]
    rows = pltpu.VMEM((count, D), jnp.bfloat16)
    (merged,) = call(
        merge_kernel, [bf16(count, D)], [rows, rows, pltpu.VMEM((8, D, D // 2), jnp.bfloat16)],
        (2 * 10**9, 8 * 10**6, 10**6), "merge", [live, block, gains, *eighths],
    )
    return merged


def after(value, *others):
    return lax.optimization_barrier((value,) + others)[0]


def assemble_kernel(*refs):
    pieces, outs = refs[:-2], refs[-2:]
    z = lax.axis_index("chan") // 2
    part = pieces[0].shape[0] // 2
    count = outs[0].shape[0] // (2 * part)

    def put(rows, d, at):
        at = lax.rem(at + 2 * count, count)
        lo = 0
        for out_ref in outs:
            width = out_ref.shape[1]
            begin = pl.multiple_of((d * count + at) * part, part)
            out_ref[pl.ds(begin, part)] = rows[:, lo : lo + width]
            lo += width

    for n, piece in enumerate(pieces[:-2]):
        step = (n + 1) // 2
        at = z - step if n % 2 else z + step
        for d in range(2):
            put(piece[d * part : (d + 1) * part], d, at)
    for d in range(2):
        put(pieces[d - 2][...], d, z + count // 2)


class WeightRing:
    def __init__(self, shard):
        dp, chan = lax.axis_index("dp"), lax.axis_index("chan")
        core, channels = chan % 2, lax.axis_size("chan")
        height, cols = shard.shape
        half = cols // 2
        mate = lax.ppermute(shard, "dp", [(0, 1), (1, 0)])
        pair = jnp.where(dp == 0, jnp.stack([shard, mate]), jnp.stack([mate, shard]))
        mine = jnp.where(core == 0, pair[..., :half], pair[..., half:])
        give = jnp.where(core == 0, pair[..., half:], pair[..., :half])
        self.swap = [(i, i ^ 1) for i in range(channels)]
        beside = lax.ppermute(give, "chan", self.swap)
        chip = jnp.where(core == 0, jnp.stack([mine, beside], 1), jnp.stack([beside, mine], 1))
        block = chip.reshape(4 * height, half)
        self.up = [(i, (i + 2) % channels) for i in range(channels)]
        self.down = [(i, (i - 2) % channels) for i in range(channels)]
        self.ends, self.pieces, self.left = (block, block), [block], channels // 4
        self.shape = (2 * channels * height, half)

    def step(self, *others):
        high, low = self.ends
        self.left -= 1
        if not self.left:
            part = high.shape[0] // 2
            high, low = high[:part], low[part:]
        high = lax.ppermute(after(high, *others) if others else high, "chan", self.up)
        low = lax.ppermute(after(low, *others) if others else low, "chan", self.down)
        self.ends = (high, low)
        self.pieces += [high, low]

    def assemble(self, split, *others):
        self.pieces[0] = after(self.pieces[0], *others)
        rows, cols = self.shape
        return call(
            assemble_kernel, [bf16(rows, split), bf16(rows, cols - split)], [],
            (0, 4 * 10**6, 0), "assemble", self.pieces,
        )


def shards(
    features, lengths, chan_valid, norm_gains, branch_qkv, branch_out, depth_taps,
    point_in, point_out, merge_qkv, merge_out,
):
    place, chan = lax.axis_index("tm"), lax.axis_index("chan")
    count = 2 * ROWS
    row = place // ROWS
    packed, spread = run_prepare(features, point_in, point_out, merge_qkv, merge_out)
    point = WeightRing(packed)
    other_row = [(i, (i + ROWS) % count) for i in range(count)]
    blocks = lax.all_to_all(spread, "tm", split_axis=0, concat_axis=0, tiled=True)
    point.step()
    point.step()
    point.step(blocks)
    context_a, norm, query, raw, group_b, group_c, wout = run_attend_a(
        lengths, blocks, norm_gains, branch_qkv, branch_out
    )
    point.step(context_a)
    context_b = run_attend_b(lengths, norm, query, group_b)
    mine, eighth = point.assemble(3 * D // 2, context_b)
    other = lax.ppermute(mine, "chan", point.swap)
    first, normed = run_attend_c(
        lengths, norm, query, raw, context_a, context_b, norm_gains, after(group_c, mine), wout
    )
    held = [eighth]
    for k in (1, 3, 2):
        pairs = [(i, i // ROWS * ROWS + (i + k) % ROWS) for i in range(count)]
        held.append(lax.ppermute(after(eighth, first), "tm", pairs))
    eighths = held + [lax.ppermute(one, "chan", point.swap) for one in held]
    kept, away = run_conv(lengths, normed, first, mine, other, depth_taps.astype(jnp.float32))
    back = lax.ppermute(away, "tm", other_row)
    second = jnp.concatenate([kept, back], axis=0)
    channels = lax.axis_size("chan")
    part = 2 * SPAN // channels
    joined = lax.all_to_all(
        second.reshape(channels, part, D), "chan", split_axis=0, concat_axis=0, tiled=True
    )
    owner = jnp.where(chan < channels // 2, row, 1 - row)
    live = jnp.repeat(chan_valid[owner], part)[None]
    merged = run_merge(live, joined.reshape(channels * part, D), norm_gains, eighths)
    returned = lax.all_to_all(
        merged.reshape(channels, part, D), "chan", split_axis=0, concat_axis=0, tiled=True
    ).reshape(2, SPAN, D)
    return jnp.where(row == 0, returned, returned[::-1])[:, None]


def solution(mesh):
    placed = (
        P("dp", "chan", "tm", None),
        P("dp"),
        P("dp", None),
        P(),
        P(),
        P(),
        P(),
        P(("dp", "chan"), None),
        P(("dp", "chan"), None),
        P(("dp", "chan"), None),
        P(("dp", "chan"), None),
    )
    return jax.shard_map(
        shards, mesh=mesh, in_specs=placed, out_specs=P("dp", "chan", "tm", None), check_vma=False
    )
```

```python
import jax
import jax.numpy as jnp
from jax import lax
from jax.experimental import pallas as pl
from jax.experimental.pallas import tpu as pltpu
from jax.sharding import PartitionSpec as P

D = 768
PAIRS = 6
SPAN = 128
PAD = 16
SEG = SPAN + 2 * PAD
FRAMES = 1024
ROWS = 4
TAPS = 31
MIB = 1024 * 1024
LOG2E = 1.4426950408889634


def normalize(values, gain):
    data = values.astype(jnp.float32)
    center = data - jnp.mean(data, axis=-1, keepdims=True)
    spread = jnp.mean(center * center, axis=-1, keepdims=True)
    return (center * lax.rsqrt(spread + 1e-05) * gain).astype(jnp.bfloat16)


def mm(left, right):
    return jnp.dot(left, right, preferred_element_type=jnp.float32)


def mm_t(left, right):
    return lax.dot_general(left, right, (((1,), (1,)), ((), ())), preferred_element_type=jnp.float32)


def pair_attention(query, key, value_ones, allowed):
    low = lax.broadcasted_iota(jnp.int32, query.shape, 1) < 64
    zero = jnp.zeros_like(query)
    outs = []
    for one in (jnp.where(low, query, zero), jnp.where(low, zero, query)):
        scores = jnp.where(allowed, mm_t(one, key), -1e30)
        top = jnp.max(scores, axis=1, keepdims=True)
        weights = jnp.exp2((scores - top) * LOG2E).astype(jnp.bfloat16)
        out = mm(weights, value_ones)
        outs.append(out[:, :128] / out[:, 128:])
    return jnp.where(low, outs[0], outs[1]).astype(jnp.bfloat16)


def bf16(*shape):
    return jax.ShapeDtypeStruct(shape, jnp.bfloat16)


def call(kernel, outs, scratch, cost, name, operands, where=None, limit=24):
    vmem = pl.BlockSpec(memory_space=pltpu.VMEM)
    flops, moved, exps = cost
    lead = [] if where is None else [where]
    return pl.pallas_call(
        kernel,
        in_specs=[pl.BlockSpec(memory_space=pltpu.SMEM)] * len(lead)
        + [pl.BlockSpec(memory_space=pltpu.HBM) if isinstance(x, Far) else vmem for x in operands],
        out_specs=[vmem] * len(outs),
        out_shape=outs,
        scratch_shapes=scratch,
        compiler_params=pltpu.CompilerParams(vmem_limit_bytes=limit * MIB),
        cost_estimate=pl.CostEstimate(flops=flops, bytes_accessed=moved, transcendentals=exps),
        name=name,
    )(*lead, *[x.array if isinstance(x, Far) else x for x in operands])


class Far:
    def __init__(self, array):
        self.array = array


def prepare_kernel(
    pin, pout, mqkv, mout, features, out_ref, spread_ref, pin_s, pout_s, mqkv_s, mout_s, sems
):
    shards_in = ((pin, pin_s), (pout, pout_s), (mqkv, mqkv_s), (mout, mout_s))
    blocks = [(features.at[t // ROWS, 0], spread_ref.at[t]) for t in range(2 * ROWS)]
    copies = [
        pltpu.make_async_copy(a, b, sems.at[n]) for n, (a, b) in enumerate((*shards_in, *blocks))
    ]
    for copy in copies:
        copy.start()
    for copy in copies[:4]:
        copy.wait()
    half = D // 2
    col = lax.rem(lax.axis_index("tm"), ROWS)
    for h in range(2):
        lo, base = h * half, h * 2 * D
        out_ref[:, base : base + half] = pin_s[:, lo : lo + half]
        out_ref[:, base + half : base + 2 * half] = pin_s[:, D + lo : D + lo + half]
        out_ref[:, base + 2 * half : base + 3 * half] = pout_s[:, lo : lo + half]

        @pl.when(col < ROWS - 1)
        def _():
            for n in range(3):
                lanes = pl.ds(pl.multiple_of(n * D + (2 * col + h) * 128, 128), 128)
                at = base + 3 * half + n * 128
                out_ref[:, at : at + 128] = mqkv_s[:, lanes]

        @pl.when(col == ROWS - 1)
        def _():
            out_ref[:, base + 3 * half : base + 4 * half] = mout_s[:, lo : lo + half]

    for copy in copies[4:]:
        copy.wait()


def run_prepare(features, *shards_in):
    height, count = shards_in[0].shape[0], 2 * ROWS
    scratch = [pltpu.VMEM(w.shape, w.dtype) for w in shards_in]
    return call(
        prepare_kernel, [bf16(height, 4 * D), bf16(count, SPAN, D)],
        scratch + [pltpu.SemaphoreType.DMA((4 + count,))],
        (0, 3 * 10**6, 0), "prepare", [Far(w) for w in (*shards_in, features)], limit=56,
    )


def my_core():
    return lax.rem(lax.axis_index("chan"), 2)


def my_length(lengths):
    return lengths[lax.axis_index("tm") // ROWS]


def attend_pairs(length, norm_s, query_s, weights, context_ref):
    allowed = lax.broadcasted_iota(jnp.int32, (1, FRAMES), 1) < length
    query_two = mm(query_s[...], weights[:, :256]).astype(jnp.bfloat16) * jnp.bfloat16(0.125)
    both = mm(norm_s[...], weights[:, 256:]).astype(jnp.bfloat16)
    for n in range(2):
        lanes = slice(n * 128, (n + 1) * 128)
        key, value = both[:, :256][:, lanes], both[:, 256:][:, lanes]
        value_ones = jnp.concatenate([value, jnp.ones_like(value)], axis=1)
        context_ref[:, lanes] = pair_attention(query_two[:, lanes], key, value_ones, allowed)


def attend_a_kernel(
    lengths, blocks, gains, qkv, wout,
    context_ref, norm_s, query_s, raw_s, group_b, group_c, wout_ref, group_a, sems,
):
    copies = []
    for n, group in enumerate((group_a, group_b, group_c)):
        for m in range(3):
            columns = pl.ds(m * D + n * 256, 256)
            copies.append((qkv.at[:, columns], group.at[:, pl.ds(m * 256, 256)]))
    copies.append((wout, wout_ref))
    copies = [pltpu.make_async_copy(a, b, sems.at[n]) for n, (a, b) in enumerate(copies)]
    for copy in copies:
        copy.start()
    for b in range(2 * ROWS):
        norm_s[b * SPAN : (b + 1) * SPAN] = normalize(blocks[b], gains[0:1])
    count = 2 * ROWS
    place = lax.axis_index("tm")
    for seg, b in enumerate((place, lax.rem(place + ROWS, count))):
        at, start = seg * SEG, b * SPAN
        before, following = jnp.maximum(b - 1, 0), jnp.minimum(b + 1, count - 1)
        raw_s[at : at + PAD] = blocks[before, SPAN - PAD :]
        raw_s[at + PAD : at + PAD + SPAN] = blocks[b]
        raw_s[at + PAD + SPAN : at + SEG] = blocks[following, :PAD]
        rows = lambda begin, size: norm_s[pl.ds(pl.multiple_of(begin, PAD), size)]
        query_s[at : at + PAD] = rows(before * SPAN + SPAN - PAD, PAD)
        query_s[at + PAD : at + PAD + SPAN] = rows(start, SPAN)
        query_s[at + PAD + SPAN : at + SEG] = rows(following * SPAN, PAD)
    for copy in copies[:3]:
        copy.wait()
    attend_pairs(my_length(lengths), norm_s, query_s, group_a, context_ref)
    for copy in copies[3:]:
        copy.wait()


def attend_b_kernel(lengths, norm_s, query_s, weights, context_ref):
    attend_pairs(my_length(lengths), norm_s, query_s, weights, context_ref)


def attend_c_kernel(
    lengths, norm_s, query_s, raw_s, context_a, context_b, gains, weights, wout,
    first_ref, normed_ref, context_c,
):
    attend_pairs(my_length(lengths), norm_s, query_s, weights, context_c)
    third = D // 3
    out = sum(
        mm(c[...], wout[n * third : (n + 1) * third])
        for n, c in enumerate((context_a, context_b, context_c))
    )
    first = (raw_s[...].astype(jnp.float32) + out).astype(jnp.bfloat16)
    first_ref[...] = first
    normed_ref[...] = normalize(first, gains[1:2])


WIDE = 2 * SEG
ATTEND_COST = (3 * 10**9, 5 * 10**6, 10**6)


def run_attend_a(lengths, blocks, gains, qkv, wout):
    group = bf16(D, D)
    return call(
        attend_a_kernel,
        [bf16(WIDE, D // 3), bf16(FRAMES, D), bf16(WIDE, D), bf16(WIDE, D), group, group, group],
        [pltpu.VMEM((D, D), jnp.bfloat16), pltpu.SemaphoreType.DMA((10,))],
        ATTEND_COST, "attend_a", [blocks, gains, Far(qkv), Far(wout)], lengths, limit=44,
    )


def run_attend_b(lengths, norm, query, weights):
    (context,) = call(
        attend_b_kernel, [bf16(WIDE, D // 3)], [], ATTEND_COST, "attend_b", [norm, query, weights], lengths,
    )
    return context


def run_attend_c(lengths, *operands):
    return call(
        attend_c_kernel, [bf16(WIDE, D)] * 2, [pltpu.VMEM((WIDE, D // 3), jnp.bfloat16)],
        ATTEND_COST, "attend_c", list(operands), lengths,
    )


def depthwise(gated, base, taps, swish_s):
    for chunk in range(PAIRS):
        lo = chunk * 128
        mixed = jnp.zeros((SPAN, 128), jnp.float32)
        for o in range(TAPS):
            begin = base + PAD - TAPS // 2 + o
            tap = taps[o : o + 1, lo : lo + 128]
            mixed = mixed + tap * gated[chunk, begin : begin + SPAN]
        swish = mixed * jax.nn.sigmoid(mixed)
        swish_s[:, lo : lo + 128] = swish.astype(jnp.bfloat16)


def project_out(swish_s, kept, core, halves, out_ref):
    for h, half in zip((core, 1 - core), halves):
        lanes = pl.ds(pl.multiple_of(h * (D // 2), 128), D // 2)
        out = kept[:, lanes].astype(jnp.float32) + mm(swish_s[...], half[:, D:])
        out_ref[:, lanes] = out.astype(jnp.bfloat16)


def conv_a_kernel(
    lengths, normed, first, mine, other, taps, out_ref, home_ref, gated_s, swish_s, kept_s
):
    place, length, core = lax.axis_index("tm"), my_length(lengths), my_core()
    lives = []
    for b in (place, lax.rem(place + ROWS, 2 * ROWS)):
        frame = b * SPAN - PAD + lax.broadcasted_iota(jnp.int32, (SEG, 1), 0)
        lives.append((frame >= 0) & (frame < length))
    live = jnp.concatenate(lives, axis=0)
    for h, half in zip((core, 1 - core), (mine, other)):
        for n in range(PAIRS // 2):
            lo = n * 128
            both = jnp.concatenate(
                [half[:, lo : lo + 128], half[:, D // 2 + lo : D // 2 + lo + 128]], axis=1
            )
            wide = mm(normed[...], both)
            gated = jnp.where(live, wide[:, :128] * jax.nn.sigmoid(wide[:, 128:]), 0.0)
            gated = gated.astype(jnp.bfloat16).astype(jnp.float32)
            chunk = h * (PAIRS // 2) + n
            home_ref[chunk] = gated[:SEG]
            gated_s[chunk] = gated[SEG:]
    depthwise(gated_s, 0, taps, swish_s)
    kept_s[...] = first[SEG + PAD : SEG + PAD + SPAN]
    project_out(swish_s, kept_s, core, (mine, other), out_ref)


def conv_b_kernel(home, first, mine, other, taps, out_ref, swish_s, kept_s):
    depthwise(home, 0, taps, swish_s)
    kept_s[...] = first[PAD : PAD + SPAN]
    project_out(swish_s, kept_s, my_core(), (mine, other), out_ref)


def run_conv(lengths, normed, first, mine, other, taps):
    gated = jax.ShapeDtypeStruct((PAIRS, SEG, 128), jnp.float32)
    block = pltpu.VMEM((SPAN, D), jnp.bfloat16)
    away, home = call(
        conv_a_kernel, [bf16(SPAN, D), gated], [pltpu.VMEM(gated.shape, jnp.float32), block, block],
        (2 * 10**9, 6 * 10**6, 10**6), "conv_a", [normed, first, mine, other, taps], lengths,
    )
    (kept,) = call(
        conv_b_kernel, [bf16(SPAN, D)], [block, block],
        (10**9, 4 * 10**6, 10**6), "conv_b", [home, first, mine, other, taps],
    )
    return kept, away


def merge_kernel(live, block, gains, *refs):
    eighths, (out_ref, norm_s, context_s, weights_s) = refs[:8], refs[8:]
    col, core = lax.rem(lax.axis_index("tm"), ROWS), my_core()
    for n, eighth in enumerate(eighths):
        k = (0, 1, 3, 2)[n % 4]
        e = 2 * lax.rem(col + ROWS - k, ROWS) + (core if n < 4 else 1 - core)
        weights_s[e] = eighth[...]
    norm_s[...] = normalize(block[...], gains[2:3])
    count = block.shape[0]
    mine = lax.broadcasted_iota(jnp.int32, (count, count), 0) & 15
    theirs = lax.broadcasted_iota(jnp.int32, (count, count), 1) & 15
    allowed = (mine == theirs) & (live[...] > 0)
    projected = [mm(norm_s[...], weights_s[p]).astype(jnp.bfloat16) for p in range(PAIRS)]
    for p, both in enumerate(projected):
        query, key, value = both[:, :128] * jnp.bfloat16(0.125), both[:, 128:256], both[:, 256:]
        value_ones = jnp.concatenate([value, jnp.ones_like(value)], axis=1)
        context_s[:, p * 128 : (p + 1) * 128] = pair_attention(query, key, value_ones, allowed)
    for n in range(2):
        lanes = slice(n * (D // 2), (n + 1) * (D // 2))
        out = block[:, lanes].astype(jnp.float32) + mm(context_s[...], weights_s[PAIRS + n])
        out_ref[:, lanes] = out.astype(jnp.bfloat16)


def run_merge(live, block, gains, eighths):
    count = block.shape[0]
    rows = pltpu.VMEM((count, D), jnp.bfloat16)
    (merged,) = call(
        merge_kernel, [bf16(count, D)], [rows, rows, pltpu.VMEM((8, D, D // 2), jnp.bfloat16)],
        (2 * 10**9, 8 * 10**6, 10**6), "merge", [live, block, gains, *eighths],
    )
    return merged


def after(value, *others):
    return lax.optimization_barrier((value,) + others)[0]


def assemble_kernel(*refs):
    pieces, outs = refs[:-2], refs[-2:]
    z = lax.axis_index("chan") // 2
    part = pieces[0].shape[0] // 2
    count = outs[0].shape[0] // (2 * part)

    def put(rows, d, at):
        at = lax.rem(at + 2 * count, count)
        lo = 0
        for out_ref in outs:
            width = out_ref.shape[1]
            begin = pl.multiple_of((d * count + at) * part, part)
            out_ref[pl.ds(begin, part)] = rows[:, lo : lo + width]
            lo += width

    for n, piece in enumerate(pieces[:-2]):
        step = (n + 1) // 2
        at = z - step if n % 2 else z + step
        for d in range(2):
            put(piece[d * part : (d + 1) * part], d, at)
    for d in range(2):
        put(pieces[d - 2][...], d, z + count // 2)


class WeightRing:
    def __init__(self, shard):
        dp, chan = lax.axis_index("dp"), lax.axis_index("chan")
        core, channels = chan % 2, lax.axis_size("chan")
        height, cols = shard.shape
        half = cols // 2
        mate = lax.ppermute(shard, "dp", [(0, 1), (1, 0)])
        pair = jnp.where(dp == 0, jnp.stack([shard, mate]), jnp.stack([mate, shard]))
        mine = jnp.where(core == 0, pair[..., :half], pair[..., half:])
        give = jnp.where(core == 0, pair[..., half:], pair[..., :half])
        self.swap = [(i, i ^ 1) for i in range(channels)]
        beside = lax.ppermute(give, "chan", self.swap)
        chip = jnp.where(core == 0, jnp.stack([mine, beside], 1), jnp.stack([beside, mine], 1))
        block = chip.reshape(4 * height, half)
        self.up = [(i, (i + 2) % channels) for i in range(channels)]
        self.down = [(i, (i - 2) % channels) for i in range(channels)]
        self.ends, self.pieces, self.left = (block, block), [block], channels // 4
        self.shape = (2 * channels * height, half)

    def step(self, *others):
        high, low = self.ends
        self.left -= 1
        if not self.left:
            part = high.shape[0] // 2
            high, low = high[:part], low[part:]
        high = lax.ppermute(after(high, *others) if others else high, "chan", self.up)
        low = lax.ppermute(after(low, *others) if others else low, "chan", self.down)
        self.ends = (high, low)
        self.pieces += [high, low]

    def assemble(self, split, *others):
        self.pieces[0] = after(self.pieces[0], *others)
        rows, cols = self.shape
        return call(
            assemble_kernel, [bf16(rows, split), bf16(rows, cols - split)], [],
            (0, 4 * 10**6, 0), "assemble", self.pieces,
        )


def shards(
    features, lengths, chan_valid, norm_gains, branch_qkv, branch_out, depth_taps,
    point_in, point_out, merge_qkv, merge_out,
):
    place, chan = lax.axis_index("tm"), lax.axis_index("chan")
    count = 2 * ROWS
    row = place // ROWS
    packed, spread = run_prepare(features, point_in, point_out, merge_qkv, merge_out)
    point = WeightRing(packed)
    other_row = [(i, (i + ROWS) % count) for i in range(count)]
    blocks = lax.all_to_all(spread, "tm", split_axis=0, concat_axis=0, tiled=True)
    point.step()
    point.step()
    point.step(blocks)
    context_a, norm, query, raw, group_b, group_c, wout = run_attend_a(
        lengths, blocks, norm_gains, branch_qkv, branch_out
    )
    point.step(context_a)
    context_b = run_attend_b(lengths, norm, query, group_b)
    mine, eighth = point.assemble(3 * D // 2, context_b)
    other = lax.ppermute(mine, "chan", point.swap)
    first, normed = run_attend_c(
        lengths, norm, query, raw, context_a, context_b, norm_gains, after(group_c, mine), wout
    )
    def beside(values, k):
        pairs = [(i, i // ROWS * ROWS + (i + k) % ROWS) for i in range(count)]
        return lax.ppermute(values, "tm", pairs)

    far = beside(eighth, 2)
    kept, away = run_conv(lengths, normed, first, mine, other, depth_taps.astype(jnp.float32))
    back = lax.ppermute(away, "tm", other_row)
    late = after(eighth, away)
    held = [eighth, beside(late, 1), beside(late, 3), far]
    eighths = held + [lax.ppermute(one, "chan", point.swap) for one in held]
    second = jnp.concatenate([kept, back], axis=0)
    channels = lax.axis_size("chan")
    part = 2 * SPAN // channels
    joined = lax.all_to_all(
        second.reshape(channels, part, D), "chan", split_axis=0, concat_axis=0, tiled=True
    )
    owner = jnp.where(chan < channels // 2, row, 1 - row)
    live = jnp.repeat(chan_valid[owner], part)[None]
    merged = run_merge(live, joined.reshape(channels * part, D), norm_gains, eighths)
    returned = lax.all_to_all(
        merged.reshape(channels, part, D), "chan", split_axis=0, concat_axis=0, tiled=True
    ).reshape(2, SPAN, D)
    return jnp.where(row == 0, returned, returned[::-1])[:, None]


def solution(mesh):
    placed = (
        P("dp", "chan", "tm", None),
        P("dp"),
        P("dp", None),
        P(),
        P(),
        P(),
        P(),
        P(("dp", "chan"), None),
        P(("dp", "chan"), None),
        P(("dp", "chan"), None),
        P(("dp", "chan"), None),
    )
    return jax.shard_map(
        shards, mesh=mesh, in_specs=placed, out_specs=P("dp", "chan", "tm", None), check_vma=False
    )
```

```python
import functools

import jax
import jax.numpy as jnp
from jax import lax
from jax.experimental import pallas as pl
from jax.experimental.pallas import tpu as pltpu
from jax.sharding import PartitionSpec as P

D = 768
PAIRS = 6
SPAN = 128
PAD = 16
SEG = SPAN + 2 * PAD
FRAMES = 1024
ROWS = 4
TAPS = 31
MIB = 1024 * 1024
LOG2E = 1.4426950408889634


def normalize(values, gain):
    data = values.astype(jnp.float32)
    center = data - jnp.mean(data, axis=-1, keepdims=True)
    spread = jnp.mean(center * center, axis=-1, keepdims=True)
    return (center * lax.rsqrt(spread + 1e-05) * gain).astype(jnp.bfloat16)


def mm(left, right):
    return jnp.dot(left, right, preferred_element_type=jnp.float32)


def mm_t(left, right):
    return lax.dot_general(left, right, (((1,), (1,)), ((), ())), preferred_element_type=jnp.float32)


def pair_attention(query, key, value_ones, allowed):
    low = lax.broadcasted_iota(jnp.int32, query.shape, 1) < 64
    zero = jnp.zeros_like(query)
    outs = []
    for one in (jnp.where(low, query, zero), jnp.where(low, zero, query)):
        scores = jnp.where(allowed, mm_t(one, key), -1e30)
        top = jnp.max(scores, axis=1, keepdims=True)
        weights = jnp.exp2((scores - top) * LOG2E).astype(jnp.bfloat16)
        out = mm(weights, value_ones)
        outs.append(out[:, :128] / out[:, 128:])
    return jnp.where(low, outs[0], outs[1]).astype(jnp.bfloat16)


def bf16(*shape):
    return jax.ShapeDtypeStruct(shape, jnp.bfloat16)


def call(kernel, outs, scratch, cost, name, operands, where=None, limit=24):
    vmem = pl.BlockSpec(memory_space=pltpu.VMEM)
    flops, moved, exps = cost
    lead = [] if where is None else [where]
    return pl.pallas_call(
        kernel,
        in_specs=[pl.BlockSpec(memory_space=pltpu.SMEM)] * len(lead)
        + [pl.BlockSpec(memory_space=pltpu.HBM) if isinstance(x, Far) else vmem for x in operands],
        out_specs=[vmem] * len(outs),
        out_shape=outs,
        scratch_shapes=scratch,
        compiler_params=pltpu.CompilerParams(vmem_limit_bytes=limit * MIB),
        cost_estimate=pl.CostEstimate(flops=flops, bytes_accessed=moved, transcendentals=exps),
        name=name,
    )(*lead, *[x.array if isinstance(x, Far) else x for x in operands])


class Far:
    def __init__(self, array):
        self.array = array


def prepare_kernel(
    pin, pout, mqkv, mout, features, out_ref, spread_ref, pin_s, pout_s, mqkv_s, mout_s, sems
):
    shards_in = ((pin, pin_s), (pout, pout_s), (mqkv, mqkv_s), (mout, mout_s))
    blocks = [(features.at[u, 0], spread_ref.at[u * ROWS]) for u in range(2)]
    copies = [
        pltpu.make_async_copy(a, b, sems.at[n]) for n, (a, b) in enumerate((*shards_in, *blocks))
    ]
    for copy in copies:
        copy.start()
    for copy in copies[:4]:
        copy.wait()
    half = D // 2
    col = lax.rem(lax.axis_index("tm"), ROWS)
    for h in range(2):
        lo, base = h * half, h * 2 * D
        out_ref[:, base : base + half] = pin_s[:, lo : lo + half]
        out_ref[:, base + half : base + 2 * half] = pin_s[:, D + lo : D + lo + half]
        out_ref[:, base + 2 * half : base + 3 * half] = pout_s[:, lo : lo + half]

        @pl.when(col < ROWS - 1)
        def _():
            for n in range(3):
                lanes = pl.ds(pl.multiple_of(n * D + (2 * col + h) * 128, 128), 128)
                at = base + 3 * half + n * 128
                out_ref[:, at : at + 128] = mqkv_s[:, lanes]

        @pl.when(col == ROWS - 1)
        def _():
            out_ref[:, base + 3 * half : base + 4 * half] = mout_s[:, lo : lo + half]

    for copy in copies[4:]:
        copy.wait()
    for t in range(2 * ROWS):
        if t % ROWS:
            spread_ref[t] = spread_ref[t // ROWS * ROWS]


def run_prepare(features, *shards_in):
    height, count = shards_in[0].shape[0], 2 * ROWS
    scratch = [pltpu.VMEM(w.shape, w.dtype) for w in shards_in]
    return call(
        prepare_kernel, [bf16(height, 4 * D), bf16(count, SPAN, D)],
        scratch + [pltpu.SemaphoreType.DMA((6,))],
        (0, 3 * 10**6, 0), "prepare", [Far(w) for w in (*shards_in, features)], limit=56,
    )


def my_core():
    return lax.rem(lax.axis_index("chan"), 2)


def my_length(lengths):
    return lengths[lax.axis_index("tm") // ROWS]


def attend_pairs(length, norm_s, query_s, weights, context_ref):
    allowed = lax.broadcasted_iota(jnp.int32, (1, FRAMES), 1) < length
    query_two = mm(query_s[...], weights[:, :256]).astype(jnp.bfloat16) * jnp.bfloat16(0.125)
    both = mm(norm_s[...], weights[:, 256:]).astype(jnp.bfloat16)
    for n in range(2):
        lanes = slice(n * 128, (n + 1) * 128)
        key, value = both[:, :256][:, lanes], both[:, 256:][:, lanes]
        value_ones = jnp.concatenate([value, jnp.ones_like(value)], axis=1)
        context_ref[:, lanes] = pair_attention(query_two[:, lanes], key, value_ones, allowed)


def attend_a_kernel(
    lengths, blocks, gains, qkv, wout,
    context_ref, norm_s, query_s, raw_s, group_b, group_c, wout_ref, group_a, sems,
):
    copies = []
    for n, group in enumerate((group_a, group_b, group_c)):
        for m in range(3):
            columns = pl.ds(m * D + n * 256, 256)
            copies.append((qkv.at[:, columns], group.at[:, pl.ds(m * 256, 256)]))
    copies.append((wout, wout_ref))
    copies = [pltpu.make_async_copy(a, b, sems.at[n]) for n, (a, b) in enumerate(copies)]
    for copy in copies:
        copy.start()
    for b in range(2 * ROWS):
        norm_s[b * SPAN : (b + 1) * SPAN] = normalize(blocks[b], gains[0:1])
    count = 2 * ROWS
    place = lax.axis_index("tm")
    for seg, b in enumerate((place, lax.rem(place + ROWS, count))):
        at, start = seg * SEG, b * SPAN
        before, following = jnp.maximum(b - 1, 0), jnp.minimum(b + 1, count - 1)
        raw_s[at : at + PAD] = blocks[before, SPAN - PAD :]
        raw_s[at + PAD : at + PAD + SPAN] = blocks[b]
        raw_s[at + PAD + SPAN : at + SEG] = blocks[following, :PAD]
        rows = lambda begin, size: norm_s[pl.ds(pl.multiple_of(begin, PAD), size)]
        query_s[at : at + PAD] = rows(before * SPAN + SPAN - PAD, PAD)
        query_s[at + PAD : at + PAD + SPAN] = rows(start, SPAN)
        query_s[at + PAD + SPAN : at + SEG] = rows(following * SPAN, PAD)
    for copy in copies[:3]:
        copy.wait()
    attend_pairs(my_length(lengths), norm_s, query_s, group_a, context_ref)
    for copy in copies[3:]:
        copy.wait()


def attend_b_kernel(lengths, norm_s, query_s, weights, context_ref):
    attend_pairs(my_length(lengths), norm_s, query_s, weights, context_ref)


def attend_c_kernel(
    lengths, norm_s, query_s, raw_s, context_a, context_b, gains, weights, wout,
    first_ref, normed_ref, context_c,
):
    attend_pairs(my_length(lengths), norm_s, query_s, weights, context_c)
    third = D // 3
    out = sum(
        mm(c[...], wout[n * third : (n + 1) * third])
        for n, c in enumerate((context_a, context_b, context_c))
    )
    first = (raw_s[...].astype(jnp.float32) + out).astype(jnp.bfloat16)
    first_ref[...] = first
    normed_ref[...] = normalize(first, gains[1:2])


WIDE = 2 * SEG
ATTEND_COST = (3 * 10**9, 5 * 10**6, 10**6)


def run_attend_a(lengths, blocks, gains, qkv, wout):
    group = bf16(D, D)
    return call(
        attend_a_kernel,
        [bf16(WIDE, D // 3), bf16(FRAMES, D), bf16(WIDE, D), bf16(WIDE, D), group, group, group],
        [pltpu.VMEM((D, D), jnp.bfloat16), pltpu.SemaphoreType.DMA((10,))],
        ATTEND_COST, "attend_a", [blocks, gains, Far(qkv), Far(wout)], lengths, limit=44,
    )


def run_attend_b(lengths, norm, query, weights):
    (context,) = call(
        attend_b_kernel, [bf16(WIDE, D // 3)], [], ATTEND_COST, "attend_b", [norm, query, weights], lengths,
    )
    return context


def run_attend_c(lengths, *operands):
    return call(
        attend_c_kernel, [bf16(WIDE, D)] * 2, [pltpu.VMEM((WIDE, D // 3), jnp.bfloat16)],
        ATTEND_COST, "attend_c", list(operands), lengths,
    )


def depthwise(gated, base, taps, swish_s):
    for chunk in range(PAIRS):
        lo = chunk * 128
        mixed = jnp.zeros((SPAN, 128), jnp.float32)
        for o in range(TAPS):
            begin = base + PAD - TAPS // 2 + o
            tap = taps[o : o + 1, lo : lo + 128]
            mixed = mixed + tap * gated[chunk, begin : begin + SPAN]
        swish = mixed * jax.nn.sigmoid(mixed)
        swish_s[:, lo : lo + 128] = swish.astype(jnp.bfloat16)


def project_out(swish_s, kept, core, halves, out_ref):
    for h, half in zip((core, 1 - core), halves):
        lanes = pl.ds(pl.multiple_of(h * (D // 2), 128), D // 2)
        out = kept[:, lanes].astype(jnp.float32) + mm(swish_s[...], half[:, D:])
        out_ref[:, lanes] = out.astype(jnp.bfloat16)


def conv_kernel(seg, lengths, normed, first, mine, other, taps, out_ref, gated_s, swish_s, kept_s):
    place, length, core = lax.axis_index("tm"), my_length(lengths), my_core()
    at = seg * SEG
    block = lax.rem(place + seg * ROWS, 2 * ROWS)
    frame = block * SPAN - PAD + lax.broadcasted_iota(jnp.int32, (SEG, 1), 0)
    live = (frame >= 0) & (frame < length)
    rows = normed[at : at + SEG]
    for h, half in zip((core, 1 - core), (mine, other)):
        wide = mm(rows, half[:, :D])
        for n in range(PAIRS // 2):
            lo = n * 128
            gate = wide[:, D // 2 + lo : D // 2 + lo + 128]
            gated = jnp.where(live, wide[:, lo : lo + 128] * jax.nn.sigmoid(gate), 0.0)
            gated_s[h * (PAIRS // 2) + n] = gated.astype(jnp.bfloat16).astype(jnp.float32)
    depthwise(gated_s, 0, taps, swish_s)
    kept_s[...] = first[at + PAD : at + PAD + SPAN]
    project_out(swish_s, kept_s, core, (mine, other), out_ref)


def run_conv(seg, lengths, *operands):
    block = pltpu.VMEM((SPAN, D), jnp.bfloat16)
    (out,) = call(
        functools.partial(conv_kernel, seg), [bf16(SPAN, D)],
        [pltpu.VMEM((PAIRS, SEG, 128), jnp.float32), block, block],
        (10**9, 6 * 10**6, 10**6), "conv", list(operands), lengths,
    )
    return out


def merge_kernel(live, block, gains, *refs):
    eighths, (out_ref, norm_s, context_s, weights_s) = refs[:8], refs[8:]
    col, core = lax.rem(lax.axis_index("tm"), ROWS), my_core()
    for n, eighth in enumerate(eighths):
        k = (0, 1, 3, 2)[n % 4]
        e = 2 * lax.rem(col + ROWS - k, ROWS) + (core if n < 4 else 1 - core)
        weights_s[e] = eighth[...]
    norm_s[...] = normalize(block[...], gains[2:3])
    count = block.shape[0]
    mine = lax.broadcasted_iota(jnp.int32, (count, count), 0) & 15
    theirs = lax.broadcasted_iota(jnp.int32, (count, count), 1) & 15
    allowed = (mine == theirs) & (live[...] > 0)
    projected = [mm(norm_s[...], weights_s[p]).astype(jnp.bfloat16) for p in range(PAIRS)]
    for p, both in enumerate(projected):
        query, key, value = both[:, :128] * jnp.bfloat16(0.125), both[:, 128:256], both[:, 256:]
        value_ones = jnp.concatenate([value, jnp.ones_like(value)], axis=1)
        context_s[:, p * 128 : (p + 1) * 128] = pair_attention(query, key, value_ones, allowed)
    for n in range(2):
        lanes = slice(n * (D // 2), (n + 1) * (D // 2))
        out = block[:, lanes].astype(jnp.float32) + mm(context_s[...], weights_s[PAIRS + n])
        out_ref[:, lanes] = out.astype(jnp.bfloat16)


def run_merge(live, block, gains, eighths):
    count = block.shape[0]
    rows = pltpu.VMEM((count, D), jnp.bfloat16)
    (merged,) = call(
        merge_kernel, [bf16(count, D)], [rows, rows, pltpu.VMEM((8, D, D // 2), jnp.bfloat16)],
        (2 * 10**9, 8 * 10**6, 10**6), "merge", [live, block, gains, *eighths],
    )
    return merged


def after(value, *others):
    return lax.optimization_barrier((value,) + others)[0]


def assemble_kernel(*refs):
    pieces, outs = refs[:-2], refs[-2:]
    z = lax.axis_index("chan") // 2
    part = pieces[0].shape[0] // 2
    count = outs[0].shape[0] // (2 * part)

    def put(rows, d, at):
        at = lax.rem(at + 2 * count, count)
        lo = 0
        for out_ref in outs:
            width = out_ref.shape[1]
            begin = pl.multiple_of((d * count + at) * part, part)
            out_ref[pl.ds(begin, part)] = rows[:, lo : lo + width]
            lo += width

    for n, piece in enumerate(pieces[:-2]):
        step = (n + 1) // 2
        at = z - step if n % 2 else z + step
        for d in range(2):
            put(piece[d * part : (d + 1) * part], d, at)
    for d in range(2):
        put(pieces[d - 2][...], d, z + count // 2)


class WeightRing:
    def __init__(self, shard):
        dp, chan = lax.axis_index("dp"), lax.axis_index("chan")
        core, channels = chan % 2, lax.axis_size("chan")
        height, cols = shard.shape
        half = cols // 2
        mate = lax.ppermute(shard, "dp", [(0, 1), (1, 0)])
        pair = jnp.where(dp == 0, jnp.stack([shard, mate]), jnp.stack([mate, shard]))
        mine = jnp.where(core == 0, pair[..., :half], pair[..., half:])
        give = jnp.where(core == 0, pair[..., half:], pair[..., :half])
        self.swap = [(i, i ^ 1) for i in range(channels)]
        beside = lax.ppermute(give, "chan", self.swap)
        chip = jnp.where(core == 0, jnp.stack([mine, beside], 1), jnp.stack([beside, mine], 1))
        block = chip.reshape(4 * height, half)
        self.up = [(i, (i + 2) % channels) for i in range(channels)]
        self.down = [(i, (i - 2) % channels) for i in range(channels)]
        self.ends, self.pieces, self.left = (block, block), [block], channels // 4
        self.shape = (2 * channels * height, half)

    def step(self, *others):
        high, low = self.ends
        self.left -= 1
        if not self.left:
            part = high.shape[0] // 2
            high, low = high[:part], low[part:]
        high = lax.ppermute(after(high, *others) if others else high, "chan", self.up)
        low = lax.ppermute(after(low, *others) if others else low, "chan", self.down)
        self.ends = (high, low)
        self.pieces += [high, low]

    def assemble(self, split, *others):
        self.pieces[0] = after(self.pieces[0], *others)
        rows, cols = self.shape
        return call(
            assemble_kernel, [bf16(rows, split), bf16(rows, cols - split)], [],
            (0, 4 * 10**6, 0), "assemble", self.pieces,
        )


def shards(
    features, lengths, chan_valid, norm_gains, branch_qkv, branch_out, depth_taps,
    point_in, point_out, merge_qkv, merge_out,
):
    place, chan = lax.axis_index("tm"), lax.axis_index("chan")
    count = 2 * ROWS
    row = place // ROWS
    packed, spread = run_prepare(features, point_in, point_out, merge_qkv, merge_out)
    point = WeightRing(packed)
    other_row = [(i, (i + ROWS) % count) for i in range(count)]
    blocks = lax.all_to_all(spread, "tm", split_axis=0, concat_axis=0, tiled=True)
    point.step()
    point.step()
    point.step(blocks)
    context_a, norm, query, raw, group_b, group_c, wout = run_attend_a(
        lengths, blocks, norm_gains, branch_qkv, branch_out
    )
    point.step(context_a)
    context_b = run_attend_b(lengths, norm, query, group_b)
    mine, eighth = point.assemble(3 * D // 2, context_b)
    other = lax.ppermute(mine, "chan", point.swap)
    first, normed = run_attend_c(
        lengths, norm, query, raw, context_a, context_b, norm_gains, after(group_c, mine), wout
    )
    def beside(values, k):
        pairs = [(i, i // ROWS * ROWS + (i + k) % ROWS) for i in range(count)]
        return lax.ppermute(values, "tm", pairs)

    held = [eighth] + [beside(after(eighth, first), k) for k in (1, 3, 2)]
    operands = (normed, first, mine, other, depth_taps.astype(jnp.float32))
    away = run_conv(1, lengths, *operands)
    back = lax.ppermute(away, "tm", other_row)
    kept = run_conv(0, lengths, after(normed, away), *operands[1:])
    eighths = held + [lax.ppermute(one, "chan", point.swap) for one in held]
    second = jnp.concatenate([kept, back], axis=0)
    channels = lax.axis_size("chan")
    part = 2 * SPAN // channels
    joined = lax.all_to_all(
        second.reshape(channels, part, D), "chan", split_axis=0, concat_axis=0, tiled=True
    )
    owner = jnp.where(chan < channels // 2, row, 1 - row)
    live = jnp.repeat(chan_valid[owner], part)[None]
    merged = run_merge(live, joined.reshape(channels * part, D), norm_gains, eighths)
    returned = lax.all_to_all(
        merged.reshape(channels, part, D), "chan", split_axis=0, concat_axis=0, tiled=True
    ).reshape(2, SPAN, D)
    return jnp.where(row == 0, returned, returned[::-1])[:, None]


def solution(mesh):
    placed = (
        P("dp", "chan", "tm", None),
        P("dp"),
        P("dp", None),
        P(),
        P(),
        P(),
        P(),
        P(("dp", "chan"), None),
        P(("dp", "chan"), None),
        P(("dp", "chan"), None),
        P(("dp", "chan"), None),
    )
    return jax.shard_map(
        shards, mesh=mesh, in_specs=placed, out_specs=P("dp", "chan", "tm", None), check_vma=False
    )
```

```python
import functools

import jax
import jax.numpy as jnp
from jax import lax
from jax.experimental import pallas as pl
from jax.experimental.pallas import tpu as pltpu
from jax.sharding import PartitionSpec as P

D = 768
PAIRS = 6
SPAN = 128
PAD = 16
SEG = SPAN + 2 * PAD
FRAMES = 1024
ROWS = 4
TAPS = 31
MIB = 1024 * 1024
LOG2E = 1.4426950408889634


def normalize(values, gain):
    data = values.astype(jnp.float32)
    center = data - jnp.mean(data, axis=-1, keepdims=True)
    spread = jnp.mean(center * center, axis=-1, keepdims=True)
    return (center * lax.rsqrt(spread + 1e-05) * gain).astype(jnp.bfloat16)


def mm(left, right):
    return jnp.dot(left, right, preferred_element_type=jnp.float32)


def mm_t(left, right):
    return lax.dot_general(left, right, (((1,), (1,)), ((), ())), preferred_element_type=jnp.float32)


def pair_attention(query, key, value_ones, allowed):
    low = lax.broadcasted_iota(jnp.int32, query.shape, 1) < 64
    zero = jnp.zeros_like(query)
    outs = []
    for one in (jnp.where(low, query, zero), jnp.where(low, zero, query)):
        scores = jnp.where(allowed, mm_t(one, key), -1e30)
        top = jnp.max(scores, axis=1, keepdims=True)
        weights = jnp.exp2((scores - top) * LOG2E).astype(jnp.bfloat16)
        out = mm(weights, value_ones)
        outs.append(out[:, :128] / out[:, 128:])
    return jnp.where(low, outs[0], outs[1]).astype(jnp.bfloat16)


def bf16(*shape):
    return jax.ShapeDtypeStruct(shape, jnp.bfloat16)


def call(kernel, outs, scratch, cost, name, operands, where=None, limit=24):
    vmem = pl.BlockSpec(memory_space=pltpu.VMEM)
    flops, moved, exps = cost
    lead = [] if where is None else [where]
    return pl.pallas_call(
        kernel,
        in_specs=[pl.BlockSpec(memory_space=pltpu.SMEM)] * len(lead)
        + [pl.BlockSpec(memory_space=pltpu.HBM) if isinstance(x, Far) else vmem for x in operands],
        out_specs=[vmem] * len(outs),
        out_shape=outs,
        scratch_shapes=scratch,
        compiler_params=pltpu.CompilerParams(vmem_limit_bytes=limit * MIB),
        cost_estimate=pl.CostEstimate(flops=flops, bytes_accessed=moved, transcendentals=exps),
        name=name,
    )(*lead, *[x.array if isinstance(x, Far) else x for x in operands])


class Far:
    def __init__(self, array):
        self.array = array


def prepare_kernel(
    pin, pout, mqkv, mout, features, out_ref, spread_ref, pin_s, pout_s, mqkv_s, mout_s, sems
):
    shards_in = ((pin, pin_s), (pout, pout_s), (mqkv, mqkv_s), (mout, mout_s))
    blocks = [(features.at[u, 0], spread_ref.at[u * ROWS]) for u in range(2)]
    copies = [
        pltpu.make_async_copy(a, b, sems.at[n]) for n, (a, b) in enumerate((*shards_in, *blocks))
    ]
    for copy in copies:
        copy.start()
    for copy in copies[:4]:
        copy.wait()
    half = D // 2
    col = lax.rem(lax.axis_index("tm"), ROWS)
    for h in range(2):
        lo, base = h * half, h * 2 * D
        out_ref[:, base : base + half] = pin_s[:, lo : lo + half]
        out_ref[:, base + half : base + 2 * half] = pin_s[:, D + lo : D + lo + half]
        out_ref[:, base + 2 * half : base + 3 * half] = pout_s[:, lo : lo + half]

        @pl.when(col < ROWS - 1)
        def _():
            for n in range(3):
                lanes = pl.ds(pl.multiple_of(n * D + (2 * col + h) * 128, 128), 128)
                at = base + 3 * half + n * 128
                out_ref[:, at : at + 128] = mqkv_s[:, lanes]

        @pl.when(col == ROWS - 1)
        def _():
            out_ref[:, base + 3 * half : base + 4 * half] = mout_s[:, lo : lo + half]

    for copy in copies[4:]:
        copy.wait()
    for t in range(2 * ROWS):
        if t % ROWS:
            spread_ref[t] = spread_ref[t // ROWS * ROWS]


def run_prepare(features, *shards_in):
    height, count = shards_in[0].shape[0], 2 * ROWS
    scratch = [pltpu.VMEM(w.shape, w.dtype) for w in shards_in]
    return call(
        prepare_kernel, [bf16(height, 4 * D), bf16(count, SPAN, D)],
        scratch + [pltpu.SemaphoreType.DMA((6,))],
        (0, 3 * 10**6, 0), "prepare", [Far(w) for w in (*shards_in, features)], limit=56,
    )


def my_core():
    return lax.rem(lax.axis_index("chan"), 2)


def my_length(lengths):
    return lengths[lax.axis_index("tm") // ROWS]


PARTS = (2, 3, 1)


def attend_pairs(length, norm_s, query_s, weights, context_ref):
    allowed = lax.broadcasted_iota(jnp.int32, (1, FRAMES), 1) < length
    width = weights.shape[1] // 3
    queries = mm(query_s[...], weights[:, :width]).astype(jnp.bfloat16) * jnp.bfloat16(0.125)
    both = mm(norm_s[...], weights[:, width:]).astype(jnp.bfloat16)
    for n in range(width // 128):
        lanes = slice(n * 128, (n + 1) * 128)
        key, value = both[:, lanes], both[:, width + n * 128 : width + (n + 1) * 128]
        value_ones = jnp.concatenate([value, jnp.ones_like(value)], axis=1)
        context_ref[:, lanes] = pair_attention(queries[:, lanes], key, value_ones, allowed)


def attend_a_kernel(
    lengths, blocks, gains, qkv, wout,
    context_ref, norm_s, query_s, raw_s, group_b, group_c, wout_ref, group_a, sems,
):
    copies = []
    for n, group in enumerate((group_a, group_b, group_c)):
        for m in range(3):
            width = PARTS[n] * 128
            columns = pl.ds(m * D + sum(PARTS[:n]) * 128, width)
            copies.append((qkv.at[:, columns], group.at[:, pl.ds(m * width, width)]))
    copies.append((wout, wout_ref))
    copies = [pltpu.make_async_copy(a, b, sems.at[n]) for n, (a, b) in enumerate(copies)]
    for copy in copies:
        copy.start()
    for b in range(2 * ROWS):
        norm_s[b * SPAN : (b + 1) * SPAN] = normalize(blocks[b], gains[0:1])
    count = 2 * ROWS
    place = lax.axis_index("tm")
    for seg, b in enumerate((place, lax.rem(place + ROWS, count))):
        at, start = seg * SEG, b * SPAN
        before, following = jnp.maximum(b - 1, 0), jnp.minimum(b + 1, count - 1)
        raw_s[at : at + PAD] = blocks[before, SPAN - PAD :]
        raw_s[at + PAD : at + PAD + SPAN] = blocks[b]
        raw_s[at + PAD + SPAN : at + SEG] = blocks[following, :PAD]
        rows = lambda begin, size: norm_s[pl.ds(pl.multiple_of(begin, PAD), size)]
        query_s[at : at + PAD] = rows(before * SPAN + SPAN - PAD, PAD)
        query_s[at + PAD : at + PAD + SPAN] = rows(start, SPAN)
        query_s[at + PAD + SPAN : at + SEG] = rows(following * SPAN, PAD)
    for copy in copies[:3]:
        copy.wait()
    attend_pairs(my_length(lengths), norm_s, query_s, group_a, context_ref)
    for copy in copies[3:]:
        copy.wait()


def attend_b_kernel(lengths, norm_s, query_s, weights, context_ref):
    attend_pairs(my_length(lengths), norm_s, query_s, weights, context_ref)


def attend_c_kernel(
    lengths, norm_s, query_s, raw_s, context_a, context_b, gains, weights, wout,
    first_ref, normed_ref, context_c,
):
    attend_pairs(my_length(lengths), norm_s, query_s, weights, context_c)
    out = sum(
        mm(c[...], wout[sum(PARTS[:n]) * 128 : sum(PARTS[: n + 1]) * 128])
        for n, c in enumerate((context_a, context_b, context_c))
    )
    first = (raw_s[...].astype(jnp.float32) + out).astype(jnp.bfloat16)
    first_ref[...] = first
    normed_ref[...] = normalize(first, gains[1:2])


WIDE = 2 * SEG
ATTEND_COST = (3 * 10**9, 5 * 10**6, 10**6)


def run_attend_a(lengths, blocks, gains, qkv, wout):
    group_a, group_b, group_c = ((D, n * 384) for n in PARTS)
    return call(
        attend_a_kernel,
        [bf16(WIDE, D // 3), bf16(FRAMES, D), bf16(WIDE, D), bf16(WIDE, D), bf16(*group_b), bf16(*group_c), bf16(D, D)],
        [pltpu.VMEM(group_a, jnp.bfloat16), pltpu.SemaphoreType.DMA((10,))],
        ATTEND_COST, "attend_a", [blocks, gains, Far(qkv), Far(wout)], lengths, limit=44,
    )


def run_attend_b(lengths, norm, query, weights):
    (context,) = call(
        attend_b_kernel, [bf16(WIDE, PARTS[1] * 128)], [], ATTEND_COST, "attend_b", [norm, query, weights], lengths,
    )
    return context


def run_attend_c(lengths, *operands):
    return call(
        attend_c_kernel, [bf16(WIDE, D)] * 2, [pltpu.VMEM((WIDE, PARTS[2] * 128), jnp.bfloat16)],
        ATTEND_COST, "attend_c", list(operands), lengths,
    )


def depthwise(gated, base, taps, swish_s):
    for chunk in range(PAIRS):
        lo = chunk * 128
        mixed = jnp.zeros((SPAN, 128), jnp.float32)
        for o in range(TAPS):
            begin = base + PAD - TAPS // 2 + o
            tap = taps[o : o + 1, lo : lo + 128]
            mixed = mixed + tap * gated[chunk, begin : begin + SPAN]
        swish = mixed * jax.nn.sigmoid(mixed)
        swish_s[:, lo : lo + 128] = swish.astype(jnp.bfloat16)


def project_out(swish_s, kept, core, halves, out_ref):
    for h, half in zip((core, 1 - core), halves):
        lanes = pl.ds(pl.multiple_of(h * (D // 2), 128), D // 2)
        out = kept[:, lanes].astype(jnp.float32) + mm(swish_s[...], half[:, D:])
        out_ref[:, lanes] = out.astype(jnp.bfloat16)


def conv_kernel(seg, lengths, normed, first, mine, other, taps, out_ref, gated_s, swish_s, kept_s):
    place, length, core = lax.axis_index("tm"), my_length(lengths), my_core()
    at = seg * SEG
    block = lax.rem(place + seg * ROWS, 2 * ROWS)
    frame = block * SPAN - PAD + lax.broadcasted_iota(jnp.int32, (SEG, 1), 0)
    live = (frame >= 0) & (frame < length)
    rows = normed[at : at + SEG]
    for h, half in zip((core, 1 - core), (mine, other)):
        wide = mm(rows, half[:, :D])
        for n in range(PAIRS // 2):
            lo = n * 128
            gate = wide[:, D // 2 + lo : D // 2 + lo + 128]
            gated = jnp.where(live, wide[:, lo : lo + 128] * jax.nn.sigmoid(gate), 0.0)
            gated_s[h * (PAIRS // 2) + n] = gated.astype(jnp.bfloat16).astype(jnp.float32)
    depthwise(gated_s, 0, taps, swish_s)
    kept_s[...] = first[at + PAD : at + PAD + SPAN]
    project_out(swish_s, kept_s, core, (mine, other), out_ref)


def run_conv(seg, lengths, *operands):
    block = pltpu.VMEM((SPAN, D), jnp.bfloat16)
    (out,) = call(
        functools.partial(conv_kernel, seg), [bf16(SPAN, D)],
        [pltpu.VMEM((PAIRS, SEG, 128), jnp.float32), block, block],
        (10**9, 6 * 10**6, 10**6), "conv", list(operands), lengths,
    )
    return out


def merge_kernel(live, block, gains, *refs):
    eighths, (out_ref, norm_s, context_s, weights_s) = refs[:8], refs[8:]
    col, core = lax.rem(lax.axis_index("tm"), ROWS), my_core()
    for n, eighth in enumerate(eighths):
        k = (0, 1, 3, 2)[n % 4]
        e = 2 * lax.rem(col + ROWS - k, ROWS) + (core if n < 4 else 1 - core)
        weights_s[e] = eighth[...]
    norm_s[...] = normalize(block[...], gains[2:3])
    count = block.shape[0]
    mine = lax.broadcasted_iota(jnp.int32, (count, count), 0) & 15
    theirs = lax.broadcasted_iota(jnp.int32, (count, count), 1) & 15
    allowed = (mine == theirs) & (live[...] > 0)
    projected = [mm(norm_s[...], weights_s[p]).astype(jnp.bfloat16) for p in range(PAIRS)]
    for p, both in enumerate(projected):
        query, key, value = both[:, :128] * jnp.bfloat16(0.125), both[:, 128:256], both[:, 256:]
        value_ones = jnp.concatenate([value, jnp.ones_like(value)], axis=1)
        context_s[:, p * 128 : (p + 1) * 128] = pair_attention(query, key, value_ones, allowed)
    for n in range(2):
        lanes = slice(n * (D // 2), (n + 1) * (D // 2))
        out = block[:, lanes].astype(jnp.float32) + mm(context_s[...], weights_s[PAIRS + n])
        out_ref[:, lanes] = out.astype(jnp.bfloat16)


def run_merge(live, block, gains, eighths):
    count = block.shape[0]
    rows = pltpu.VMEM((count, D), jnp.bfloat16)
    (merged,) = call(
        merge_kernel, [bf16(count, D)], [rows, rows, pltpu.VMEM((8, D, D // 2), jnp.bfloat16)],
        (2 * 10**9, 8 * 10**6, 10**6), "merge", [live, block, gains, *eighths],
    )
    return merged


def after(value, *others):
    return lax.optimization_barrier((value,) + others)[0]


def assemble_kernel(*refs):
    pieces, outs = refs[:-2], refs[-2:]
    z = lax.axis_index("chan") // 2
    part = pieces[0].shape[0] // 2
    count = outs[0].shape[0] // (2 * part)

    def put(rows, d, at):
        at = lax.rem(at + 2 * count, count)
        lo = 0
        for out_ref in outs:
            width = out_ref.shape[1]
            begin = pl.multiple_of((d * count + at) * part, part)
            out_ref[pl.ds(begin, part)] = rows[:, lo : lo + width]
            lo += width

    for n, piece in enumerate(pieces[:-2]):
        step = (n + 1) // 2
        at = z - step if n % 2 else z + step
        for d in range(2):
            put(piece[d * part : (d + 1) * part], d, at)
    for d in range(2):
        put(pieces[d - 2][...], d, z + count // 2)


class WeightRing:
    def __init__(self, shard):
        dp, chan = lax.axis_index("dp"), lax.axis_index("chan")
        core, channels = chan % 2, lax.axis_size("chan")
        height, cols = shard.shape
        half = cols // 2
        mate = lax.ppermute(shard, "dp", [(0, 1), (1, 0)])
        pair = jnp.where(dp == 0, jnp.stack([shard, mate]), jnp.stack([mate, shard]))
        mine = jnp.where(core == 0, pair[..., :half], pair[..., half:])
        give = jnp.where(core == 0, pair[..., half:], pair[..., :half])
        self.swap = [(i, i ^ 1) for i in range(channels)]
        beside = lax.ppermute(give, "chan", self.swap)
        chip = jnp.where(core == 0, jnp.stack([mine, beside], 1), jnp.stack([beside, mine], 1))
        block = chip.reshape(4 * height, half)
        self.up = [(i, (i + 2) % channels) for i in range(channels)]
        self.down = [(i, (i - 2) % channels) for i in range(channels)]
        self.ends, self.pieces, self.left = (block, block), [block], channels // 4
        self.shape = (2 * channels * height, half)

    def step(self, *others):
        high, low = self.ends
        self.left -= 1
        if not self.left:
            part = high.shape[0] // 2
            high, low = high[:part], low[part:]
        high = lax.ppermute(after(high, *others) if others else high, "chan", self.up)
        low = lax.ppermute(after(low, *others) if others else low, "chan", self.down)
        self.ends = (high, low)
        self.pieces += [high, low]

    def assemble(self, split, *others):
        self.pieces[0] = after(self.pieces[0], *others)
        rows, cols = self.shape
        return call(
            assemble_kernel, [bf16(rows, split), bf16(rows, cols - split)], [],
            (0, 4 * 10**6, 0), "assemble", self.pieces,
        )


def shards(
    features, lengths, chan_valid, norm_gains, branch_qkv, branch_out, depth_taps,
    point_in, point_out, merge_qkv, merge_out,
):
    place, chan = lax.axis_index("tm"), lax.axis_index("chan")
    count = 2 * ROWS
    row = place // ROWS
    packed, spread = run_prepare(features, point_in, point_out, merge_qkv, merge_out)
    point = WeightRing(packed)
    other_row = [(i, (i + ROWS) % count) for i in range(count)]
    blocks = lax.all_to_all(spread, "tm", split_axis=0, concat_axis=0, tiled=True)
    point.step()
    point.step()
    point.step(blocks)
    context_a, norm, query, raw, group_b, group_c, wout = run_attend_a(
        lengths, blocks, norm_gains, branch_qkv, branch_out
    )
    point.step(context_a)
    context_b = run_attend_b(lengths, norm, query, group_b)
    mine, eighth = point.assemble(3 * D // 2, context_b)
    other = lax.ppermute(mine, "chan", point.swap)
    first, normed = run_attend_c(
        lengths, norm, query, raw, context_a, context_b, norm_gains, after(group_c, mine), wout
    )
    def beside(values, k):
        pairs = [(i, i // ROWS * ROWS + (i + k) % ROWS) for i in range(count)]
        return lax.ppermute(values, "tm", pairs)

    held = [eighth] + [beside(after(eighth, first), k) for k in (1, 3, 2)]
    operands = (normed, first, mine, other, depth_taps.astype(jnp.float32))
    away = run_conv(1, lengths, *operands)
    back = lax.ppermute(away, "tm", other_row)
    kept = run_conv(0, lengths, after(normed, away), *operands[1:])
    eighths = held + [lax.ppermute(one, "chan", point.swap) for one in held]
    second = jnp.concatenate([kept, back], axis=0)
    channels = lax.axis_size("chan")
    part = 2 * SPAN // channels
    joined = lax.all_to_all(
        second.reshape(channels, part, D), "chan", split_axis=0, concat_axis=0, tiled=True
    )
    owner = jnp.where(chan < channels // 2, row, 1 - row)
    live = jnp.repeat(chan_valid[owner], part)[None]
    merged = run_merge(live, joined.reshape(channels * part, D), norm_gains, eighths)
    returned = lax.all_to_all(
        merged.reshape(channels, part, D), "chan", split_axis=0, concat_axis=0, tiled=True
    ).reshape(2, SPAN, D)
    return jnp.where(row == 0, returned, returned[::-1])[:, None]


def solution(mesh):
    placed = (
        P("dp", "chan", "tm", None),
        P("dp"),
        P("dp", None),
        P(),
        P(),
        P(),
        P(),
        P(("dp", "chan"), None),
        P(("dp", "chan"), None),
        P(("dp", "chan"), None),
        P(("dp", "chan"), None),
    )
    return jax.shard_map(
        shards, mesh=mesh, in_specs=placed, out_specs=P("dp", "chan", "tm", None), check_vma=False
    )
```
